32 devices in a mesh: tm: 4 (over z), sx: 2 (over core), sy: 4 (over y, x).
Axes of the slice: x: 2, y: 2, z: 4, core: 2. Of those that a mesh axis runs over, the one named last changes fastest.
Arguments:
- initial: float32 [2, 4, 5, 64, 128], P('sx', 'sy'), may hold values from -6 to 6
- viscosity: float32 [2, 4, 128], P('sx', 'sy'), may hold values from 0.5 to 5
- flux_jacobian: float32 [3, 5, 5], replicated, may hold values from -2 to 2
Outputs:
- nodes: float32 [4, 3, 2, 4, 5, 64, 128], P('tm', None, 'sx', 'sy')
The draws below stay inside these ranges and needn't reach their ends.
All inputs are finite; a program needn't handle non-finite values.
Results may differ from the reference program's by a relative error of at most 0.0001.
Values sent between devices are 32-bit elements; how exact they have to be, the bound alone decides.
No kernel may reach another device: no remote copies, remote signals or barrier semaphores. Data moves between devices by JAX's collectives and lax.ppermute only.
A program may use at most 64 MiB of HBM per device.

```python
import math
import jax
import jax.numpy as jnp
from jax import lax

FIELDS = 5
NODES = 64
EZ = 128
ITERS = 2
JF = 3
JC = 2
NTIME = 4
NXE = 2
NYE = 4


def steps_of(stream_key, shape, pieces, smallest, high):
    def one(dim, shards_of):
        heights = jax.random.uniform(jax.random.fold_in(jax.random.fold_in(stream_key, 6), dim), (shards_of,), jnp.float32, smallest / len(pieces), high / len(pieces))
        return jnp.repeat(jnp.exp(heights), shape[dim] // shards_of).reshape((-1,) + (1,) * (len(shape) - dim - 1))

    loudness = one(*pieces[0])
    for cut in pieces[1:]:
        loudness = loudness * one(*cut)
    return loudness


def noise(own_key, extent, scale, bound, pieces=(), kind=jnp.bfloat16):
    loudness = steps_of(own_key, extent, pieces, -0.22, 0.18) if pieces else 1.0
    entries = jax.random.normal(own_key, extent, jnp.float32) * scale * loudness
    return jnp.minimum(jnp.maximum(entries, -bound), bound).astype(kind)


def setup_inputs(seed: int = 0) -> dict:
    arg_keys = jax.random.split(jax.random.key(seed), 4)
    initial = noise(arg_keys[0], (NXE, NYE, FIELDS, NODES, EZ), 1.0, 6.0, ((0, 2), (1, 4)), jnp.float32)
    viscosity = jnp.clip(jnp.exp(math.log(5.0) - 2.3025851 * jax.random.uniform(arg_keys[1], (NXE, NYE, EZ), jnp.float32) ** steps_of(arg_keys[1], (NXE, NYE, EZ), ((0, 2), (1, 4)), -0.2, 0.2)), 0.5, 5.0)
    flux_jacobian = noise(arg_keys[2], (3, FIELDS, FIELDS), 0.35, 2.0, (), jnp.float32)
    return {"initial": initial, "viscosity": viscosity, "flux_jacobian": flux_jacobian}


SIGMA = 3.0
BETA = 0.5
STEP = 0.1
HALF_STEP = 0.05
TWO_THIRDS = 2.0 / 3.0
ONE_THIRD = 1.0 / 3.0
HIGHEST = lax.Precision.HIGHEST
WEIGHTS = ((5.0 / 24.0, 1.0 / 3.0, -1.0 / 24.0), (-1.0 / 24.0, 1.0 / 3.0, 5.0 / 24.0))

def kron_three(first, second, third):
    return jnp.kron(jnp.kron(first, second), third)

def node_tables():
    places = jnp.arange(4)
    row = places[:, None]
    column = places[None, :]
    identity = (row == column).astype(jnp.float32)
    upper = (row + 1 == column).astype(jnp.float32)
    border = identity * ((row == 0) | (row == 3)).astype(jnp.float32)
    line_laplace = 2.0 * identity - upper - upper.T - border
    line_grad = 0.5 * upper - 0.5 * upper.T
    laplace = kron_three(line_laplace, identity, identity) + kron_three(identity, line_laplace, identity) + kron_three(identity, identity, line_laplace) + SIGMA * jnp.eye(64, dtype=jnp.float32)
    grads = jnp.stack([kron_three(line_grad, identity, identity), kron_three(identity, line_grad, identity), kron_three(identity, identity, line_grad)])
    weighting = jnp.where(row == 0, 0.5, math.sqrt(0.5)).astype(jnp.float32)
    cosine = weighting * jnp.cos(math.pi * row.astype(jnp.float32) * (2.0 * column.astype(jnp.float32) + 1.0) / 8.0)
    basis = kron_three(cosine, cosine, cosine)
    line_eigen = 2.0 - 2.0 * jnp.cos(math.pi * places.astype(jnp.float32) / 4.0)
    spectrum = (line_eigen[:, None, None] + line_eigen[None, :, None] + line_eigen[None, None, :]).reshape(64) + SIGMA
    return (laplace, grads, basis, spectrum)

def previous(array, axis):
    widths = [(0, 0)] * array.ndim
    widths[axis] = (1, 0)
    return lax.slice_in_dim(jnp.pad(array, widths), 0, array.shape[axis], axis=axis)

def following(array, axis):
    widths = [(0, 0)] * array.ndim
    widths[axis] = (0, 1)
    return lax.slice_in_dim(jnp.pad(array, widths), 1, array.shape[axis] + 1, axis=axis)

def place(before, after, axis):
    empty = jnp.zeros_like(before)
    return jnp.stack([before, empty, empty, after], axis=axis)

def neighbours(field):
    lattice = field.reshape(field.shape[:4] + (4, 4, 4) + field.shape[-1:])
    along_x = place(previous(lattice[:, :, :, :, 3], 1), following(lattice[:, :, :, :, 0], 1), 4)
    along_y = place(previous(lattice[:, :, :, :, :, 3], 2), following(lattice[:, :, :, :, :, 0], 2), 5)
    along_z = place(previous(lattice[..., 3, :], 6), following(lattice[..., 0, :], 6), 6)
    return (along_x + along_y + along_z).reshape(field.shape)

def apply_operator(field, coeff, flux_jacobian, laplace, grads, coupled):
    volume = jnp.einsum('mn,bxyfnz->bxyfmz', laplace, field, precision=HIGHEST)
    slopes = jnp.einsum('dmn,bxyfnz->dbxyfmz', grads, field, precision=HIGHEST)
    transport = jnp.einsum('dgf,dbxyfmz->bxygmz', flux_jacobian, slopes, precision=HIGHEST)
    return coeff * (volume - BETA * coupled) + transport

def precondition(residue, coeff, basis, spectrum, step):
    inverse = 1.0 / (1.0 + step * coeff * spectrum[:, None])
    modes = jnp.einsum('kn,bxyfnz->bxyfkz', basis, residue, precision=HIGHEST)
    return jnp.einsum('kn,bxyfkz->bxyfnz', basis, modes * inverse, precision=HIGHEST)

def block_jacobi(target, begin, force, step, turns, operate, solve):
    field = begin
    image = -force
    for turn in range(turns):
        if turn > 0:
            image = operate(field)
        field = field + solve(target - field - step * image, step)
    return field

def reference(initial, viscosity, flux_jacobian):
    laplace, grads, basis, spectrum = node_tables()
    coeff = viscosity[None, :, :, None, None, :]

    def operate(field):
        return apply_operator(field, coeff, flux_jacobian, laplace, grads, neighbours(field))

    def solve(residue, step):
        return precondition(residue, coeff, basis, spectrum, step)
    start = initial[None]
    force_zero = -operate(start)
    values = jnp.broadcast_to(initial, (NTIME, 3) + initial.shape)
    forces = jnp.broadcast_to(force_zero[0], (NTIME, 3) + initial.shape)

    def sweep_slice(pair):
        slice_values, slice_forces = pair
        points = [slice_values[m][None] for m in range(3)]
        old = [slice_forces[m][None] for m in range(3)]
        fresh = list(old)
        for node in range(2):
            weight = WEIGHTS[node]
            integral = STEP * (weight[0] * old[0] + weight[1] * old[1] + weight[2] * old[2])
            target = points[node] - HALF_STEP * old[node + 1] + integral
            points[node + 1] = block_jacobi(target, points[node + 1], old[node + 1], HALF_STEP, JF, operate, solve)
            fresh[node + 1] = -operate(points[node + 1])
        return (jnp.concatenate(points, axis=0), jnp.concatenate(fresh, axis=0))

    def pair_forces(pair):
        return -operate(jnp.stack(pair, axis=0))
    for sweep in range(ITERS):
        values, forces = lax.map(sweep_slice, (values, forces))
        correction = STEP * (TWO_THIRDS * forces[:, 1] - ONE_THIRD * forces[:, 0] - ONE_THIRD * forces[:, 2])
        offsets = -STEP * forces[:, 2] + HALF_STEP * (forces[:, 0] + forces[:, 2]) + correction

        def chain_turn(coarse_start, item):
            offset, end_value, end_force = item
            coarse_end = block_jacobi(coarse_start + offset[None], end_value[None], end_force[None], STEP, JC, operate, solve)
            return (coarse_end, (coarse_start[0], coarse_end[0]))
        final_end, (starts, ends) = lax.scan(chain_turn, start, (offsets, values[:, 2], forces[:, 2]))
        if sweep + 1 < ITERS:
            both = lax.map(pair_forces, (starts, ends))
            delta_start = both[:, 0] - forces[:, 0]
            delta_end = both[:, 1] - forces[:, 2]
            forces = jnp.stack([forces[:, 0] + delta_start, forces[:, 1] + 0.5 * (delta_start + delta_end), forces[:, 2] + delta_end], axis=1)
        move_start = starts - values[:, 0]
        move_end = ends - values[:, 2]
        values = jnp.stack([values[:, 0] + move_start, values[:, 1] + 0.5 * (move_start + move_end), values[:, 2] + move_end], axis=1)
    return values
```

```python
import math

import jax
import jax.numpy as jnp
import numpy as np
from jax import lax
from jax.experimental import pallas as pl
from jax.experimental.pallas import tpu as pltpu
from jax.sharding import PartitionSpec as P

ITERS = 2
JF = 3
JC = 2


SIGMA = 3.0
BETA = 0.5
STEP = 0.1
HALF_STEP = 0.05
TWO_THIRDS = 2.0 / 3.0
ONE_THIRD = 1.0 / 3.0
HIGHEST = lax.Precision.HIGHEST
WEIGHTS = ((5.0 / 24.0, 1.0 / 3.0, -1.0 / 24.0), (-1.0 / 24.0, 1.0 / 3.0, 5.0 / 24.0))


def passed_along(block, axis, distance):
    devices = range(lax.axis_size(axis))
    route = [(i - distance, i) for i in devices if i - distance in devices]
    return lax.ppermute(block, axis, route)


def kron_three(first, second, third):
    return jnp.kron(jnp.kron(first, second), third)


def node_tables():
    places = jnp.arange(4)
    row = places[:, None]
    column = places[None, :]
    identity = (row == column).astype(jnp.float32)
    upper = (row + 1 == column).astype(jnp.float32)
    border = identity * ((row == 0) | (row == 3)).astype(jnp.float32)
    line_laplace = 2.0 * identity - upper - upper.T - border
    line_grad = 0.5 * upper - 0.5 * upper.T
    laplace = (
        kron_three(line_laplace, identity, identity)
        + kron_three(identity, line_laplace, identity)
        + kron_three(identity, identity, line_laplace)
        + SIGMA * jnp.eye(64, dtype=jnp.float32)
    )
    grads = jnp.stack(
        [
            kron_three(line_grad, identity, identity),
            kron_three(identity, line_grad, identity),
            kron_three(identity, identity, line_grad),
        ]
    )
    weighting = jnp.where(row == 0, 0.5, math.sqrt(0.5)).astype(jnp.float32)
    cosine = weighting * jnp.cos(
        math.pi * row.astype(jnp.float32) * (2.0 * column.astype(jnp.float32) + 1.0) / 8.0
    )
    basis = kron_three(cosine, cosine, cosine)
    line_eigen = 2.0 - 2.0 * jnp.cos(math.pi * places.astype(jnp.float32) / 4.0)
    spectrum = (
        line_eigen[:, None, None] + line_eigen[None, :, None] + line_eigen[None, None, :]
    ).reshape(64) + SIGMA
    return (laplace, grads, basis, spectrum)


def previous(array, axis):
    widths = [(0, 0)] * array.ndim
    widths[axis] = (1, 0)
    return lax.slice_in_dim(jnp.pad(array, widths), 0, array.shape[axis], axis=axis)


def following(array, axis):
    widths = [(0, 0)] * array.ndim
    widths[axis] = (0, 1)
    return lax.slice_in_dim(jnp.pad(array, widths), 1, array.shape[axis] + 1, axis=axis)


def place(before, after, axis):
    empty = jnp.zeros_like(before)
    return jnp.stack([before, empty, empty, after], axis=axis)


def neighbours(field):
    lattice = field.reshape(field.shape[:4] + (4, 4, 4) + field.shape[-1:])
    high_x = lattice[:, :, :, :, 3]
    low_x = lattice[:, :, :, :, 0]
    from_west = passed_along(high_x[:, -1], "sx", 1)
    from_east = passed_along(low_x[:, 0], "sx", -1)
    before_x = jnp.concatenate([from_west[:, None], high_x[:, :-1]], axis=1)
    after_x = jnp.concatenate([low_x[:, 1:], from_east[:, None]], axis=1)
    high_y = lattice[:, :, :, :, :, 3]
    low_y = lattice[:, :, :, :, :, 0]
    from_south = passed_along(high_y[:, :, -1], "sy", 1)
    from_north = passed_along(low_y[:, :, 0], "sy", -1)
    before_y = jnp.concatenate([from_south[:, :, None], high_y[:, :, :-1]], axis=2)
    after_y = jnp.concatenate([low_y[:, :, 1:], from_north[:, :, None]], axis=2)
    along_x = place(before_x, after_x, 4)
    along_y = place(before_y, after_y, 5)
    along_z = place(previous(lattice[..., 3, :], 6), following(lattice[..., 0, :], 6), 6)
    return (along_x + along_y + along_z).reshape(field.shape)


def apply_operator(field, coeff, flux_jacobian, laplace, grads, coupled):
    volume = jnp.einsum("mn,bxyfnz->bxyfmz", laplace, field, precision=HIGHEST)
    slopes = jnp.einsum("dmn,bxyfnz->dbxyfmz", grads, field, precision=HIGHEST)
    transport = jnp.einsum("dgf,dbxyfmz->bxygmz", flux_jacobian, slopes, precision=HIGHEST)
    return coeff * (volume - BETA * coupled) + transport


def precondition(residue, coeff, basis, spectrum, step):
    inverse = 1.0 / (1.0 + step * coeff * spectrum[:, None])
    modes = jnp.einsum("kn,bxyfnz->bxyfkz", basis, residue, precision=HIGHEST)
    return jnp.einsum("kn,bxyfkz->bxyfnz", basis, modes * inverse, precision=HIGHEST)


def block_jacobi(target, begin, force, step, turns, operate, solve):
    field = begin
    image = -force
    for turn in range(turns):
        if turn > 0:
            image = operate(field)
        field = field + solve(target - field - step * image, step)
    return field


def local_exchanging(initial, viscosity, flux_jacobian):
    laplace, grads, basis, spectrum = node_tables()
    coeff = viscosity[None, :, :, None, None, :]
    first_slice = lax.axis_index("tm") == 0

    def operate(field):
        return apply_operator(field, coeff, flux_jacobian, laplace, grads, neighbours(field))

    def solve(residue, step):
        return precondition(residue, coeff, basis, spectrum, step)

    start = initial[None]
    force_zero = -operate(start)
    values = [start, start, start]
    forces = [force_zero, force_zero, force_zero]
    for sweep in range(ITERS):
        old = list(forces)
        for node in range(2):
            weight = WEIGHTS[node]
            integral = STEP * (weight[0] * old[0] + weight[1] * old[1] + weight[2] * old[2])
            target = values[node] - HALF_STEP * old[node + 1] + integral
            values[node + 1] = block_jacobi(
                target, values[node + 1], old[node + 1], HALF_STEP, JF, operate, solve
            )
            forces[node + 1] = -operate(values[node + 1])
        correction = STEP * (TWO_THIRDS * forces[1] - ONE_THIRD * forces[0] - ONE_THIRD * forces[2])
        offset = -STEP * forces[2] + HALF_STEP * (forces[0] + forces[2]) + correction
        end_value = values[2]
        end_force = forces[2]

        def chain_turn(turn, carry):
            coarse_start, coarse_end = carry
            coarse_end = block_jacobi(
                coarse_start + offset, end_value, end_force, STEP, JC, operate, solve
            )
            passed = passed_along(coarse_end, "tm", 1)
            return (jnp.where(first_slice, start, passed), coarse_end)

        coarse_start, coarse_end = lax.fori_loop(0, lax.axis_size("tm"), chain_turn, (start, start))
        if sweep + 1 < ITERS:
            both = -operate(jnp.concatenate([coarse_start, coarse_end], axis=0))
            force_start = both[:1]
            force_end = both[1:]
            delta_start = force_start - forces[0]
            delta_end = force_end - forces[2]
            forces = [
                forces[0] + delta_start,
                forces[1] + 0.5 * (delta_start + delta_end),
                forces[2] + delta_end,
            ]
        move_start = coarse_start - values[0]
        move_end = coarse_end - values[2]
        values = [
            values[0] + move_start,
            values[1] + 0.5 * (move_start + move_end),
            values[2] + move_end,
        ]
    return jnp.stack(values, axis=1)


FIELDS = 5
ROWS = 320
SIZE = 2560
FACE = np.array([0.5] + [math.sqrt(0.5) * math.cos(math.pi * k / 8.0) for k in (1, 2, 3)])
PICK_1 = 4.0 * FACE[1] ** 2
PICK_3 = 4.0 * FACE[3] ** 2
MODES = [
    (a, b, c)
    for parity in (0, 1)
    for a in range(4)
    for b in range(4)
    for c in range(4)
    if (a + b + c) % 2 == parity
]
PLACE = {mode: (i // 32) * 160 + i % 32 for i, mode in enumerate(MODES)}
LEVELS = sorted({tuple(sorted(mode)) for mode in MODES})


def level(a, b, c):
    return LEVELS.index(tuple(sorted((a, b, c))))


def eigen(levels):
    line = [2.0 - 2.0 * math.cos(math.pi * k / 4.0) for k in range(4)]
    return sum(line[k] for k in levels) + SIGMA


def modal_tables():
    j = np.arange(4)
    cosine = np.cos(math.pi * j[:, None] * (2.0 * j[None, :] + 1.0) / 8.0)
    cosine *= np.where(j == 0, 0.5, math.sqrt(0.5))[:, None]
    basis = np.kron(np.kron(cosine, cosine), cosine)
    scale = np.kron(np.kron(FACE, FACE), FACE)
    order = [16 * a + 4 * b + c for a, b, c in MODES]
    into = (basis / scale[:, None])[order]
    back = (basis * scale[:, None])[order].T
    upper = np.eye(4, k=1)
    slope = 0.5 * upper - 0.5 * upper.T
    one = np.eye(4)
    grads = [
        np.kron(np.kron(slope, one), one),
        np.kron(np.kron(one, slope), one),
        np.kron(np.kron(one, one), slope),
    ]
    modal = np.stack([into @ grad @ back for grad in grads])
    blocks = np.stack([modal[:, 32:, :32], modal[:, :32, 32:]])
    return into, back, HALF_STEP * blocks


def three_pass(matrix):
    high = matrix.astype(jnp.bfloat16)
    low = (matrix - high.astype(np.float64)).astype(jnp.bfloat16)
    return jnp.asarray(np.concatenate([high, low, high], axis=1))


def split_rows(x):
    high = x.astype(jnp.bfloat16)
    low = (x - high.astype(jnp.float32)).astype(jnp.bfloat16)
    return jnp.concatenate([high, high, low], axis=0)


def steps(slices):
    start, temps = 0, 6 * slices + 2
    value = 4 * slices + 2
    work, first, mid, quad, base, zed, c0, hga = range(temps, temps + 8)
    plan = [(0, start, 0), (1, work, 0), (2, work, 0), (3, work, 0), (4, work, 0), (5, work, 0)]
    plan += [(6, mid, 0)]
    for t in range(slices):
        plan += [(7, work, t), (8, t + 1, t)]
    for kind in (9, 10, 9, 11):
        plan += [(kind, value + t, t) for t in range(slices)]
    plan += [(12, value + t, t) for t in reversed(range(slices))]
    plan += [(13, work, t) for t in range(slices)]
    return plan


def whole_grid_kernel(slices, plan, where, *refs):
    gathered, refs = refs[:8], refs[8:]
    matrix, into, back, out, st, tr, g, m, dh, dd, el, cc = refs
    f32 = jnp.float32
    slot_g = slices + 1
    slot_t = 2 * slices + 2
    slot_p = 3 * slices + 2
    slot_v = 4 * slices + 2
    slot_u = 5 * slices + 2
    work, first, mid, quad, base, zed, c0, hga = range(6 * slices + 2, 6 * slices + 10)

    for k in range(8):
        cc[pl.ds(where[2 + k], 1), :] = gathered[k][320:321, :]
    visc = cc[...]
    for i, levels in enumerate(LEVELS):
        lam = (HALF_STEP * eigen(levels)) * visc
        el[8 * i : 8 * i + 8, :] = lam
        dh[8 * i : 8 * i + 8, :] = 1.0 / (1.0 + lam)
        dd[8 * i : 8 * i + 8, :] = 1.0 / (1.0 + 2.0 * lam)
    for p in range(2):
        whole = matrix[p]
        high = whole.astype(jnp.bfloat16).astype(f32)
        lane = lax.broadcasted_iota(jnp.int32, whole.shape, 1)
        middle = (lane >= 160) & (lane < 320)
        m[p] = jnp.where(middle, whole - high, high).astype(jnp.bfloat16)
    for k in range(0, 8, 2):
        for f in range(FIELDS):
            x = jnp.concatenate([gathered[k + i][64 * f : 64 * f + 64, :] for i in (0, 1)], axis=1)
            r = jnp.dot(into[...], split_rows(x), preferred_element_type=f32)
            for i in (0, 1):
                for p in (0, 1):
                    at = p * 1280 + f * 256 + where[2 + k + i]
                    st[pl.ds(at, 32, 8), :] = r[32 * p : 32 * p + 32, 128 * i : 128 * i + 128]

    sub = lax.broadcasted_iota(jnp.int32, (8, 128), 0)
    lane = lax.broadcasted_iota(jnp.int32, (8, 128), 1)
    tau = jnp.where(sub >= 4, 1.0, -1.0).astype(f32)
    y_first, y_last = sub % 4 == 0, sub % 4 == 3
    z_first, z_last = lane == 0, lane == 127
    scaled = (HALF_STEP * BETA * 0.25) * visc

    def transport(src):
        at = src * SIZE

        def pair(jp, carry):
            for p in range(2):
                begin = at + p * 1280 + 2 * jp
                x = jnp.concatenate([st[pl.ds(begin + i, 160, 8), :] for i in (0, 1)], axis=1)
                r = jnp.dot(m[p], split_rows(x), preferred_element_type=f32)
                for i in (0, 1):
                    tr[pl.ds((1 - p) * 1280 + 2 * jp + i, 160, 8), :] = r[:, 128 * i : 128 * i + 128]
            return carry

        lax.fori_loop(0, 4, pair, 0)

    def faces(src):
        def field(f, carry):
            at = pl.multiple_of(src * SIZE + f * 256, 256)
            gat = pl.multiple_of(f * 128, 128)

            def ld(a, b, c):
                return st[pl.ds(at + 8 * PLACE[a, b, c], 8), :]

            for p in range(4):
                for q in range(4):
                    i = 8 * (4 * p + q)
                    even = ld(0, p, q) + ld(2, p, q)
                    odd = PICK_1 * ld(1, p, q) + PICK_3 * ld(3, p, q)
                    met = pltpu.roll(even + tau * odd, 4, 0)
                    g[pl.ds(gat + i, 8), :] = met
                    g[pl.ds(gat + 640 + i, 8), :] = tau * met
                    even = ld(p, 0, q) + ld(p, 2, q)
                    odd = PICK_1 * ld(p, 1, q) + PICK_3 * ld(p, 3, q)
                    low = jnp.where(y_first, 0.0, pltpu.roll(even - odd, 1, 0))
                    high = jnp.where(y_last, 0.0, pltpu.roll(even + odd, 7, 0))
                    g[pl.ds(gat + 1280 + i, 8), :] = low + high
                    g[pl.ds(gat + 1920 + i, 8), :] = low - high
                    even = ld(p, q, 0) + ld(p, q, 2)
                    odd = PICK_1 * ld(p, q, 1) + PICK_3 * ld(p, q, 3)
                    low = jnp.where(z_first, 0.0, pltpu.roll(even - odd, 1, 1))
                    high = jnp.where(z_last, 0.0, pltpu.roll(even + odd, 127, 1))
                    g[pl.ds(gat + 2560 + i, 8), :] = low + high
                    g[pl.ds(gat + 3200 + i, 8), :] = low - high
            return carry

        lax.fori_loop(0, FIELDS, field, 0)

    def finish(store):
        def field(f, carry):
            at = pl.multiple_of(f * 256, 256)
            gat = pl.multiple_of(f * 128, 128)
            for pa in range(2):
                for pb in range(2):
                    gx = {
                        (b, c): g[pl.ds(gat + 640 * pa + 8 * (4 * b + c), 8), :]
                        for b in (pb, pb + 2)
                        for c in range(4)
                    }
                    gy = {
                        (a, c): g[pl.ds(gat + 1280 + 640 * pb + 8 * (4 * a + c), 8), :]
                        for a in (pa, pa + 2)
                        for c in range(4)
                    }
                    for a in (pa, pa + 2):
                        for b in (pb, pb + 2):
                            gz = [
                                g[pl.ds(gat + 2560 + 640 * pc + 8 * (4 * a + b), 8), :]
                                for pc in range(2)
                            ]
                            for c in range(4):
                                row = at + 8 * PLACE[a, b, c]
                                n = gx[b, c] + gy[a, c] + gz[c % 2]
                                image = tr[pl.ds(row, 8), :] - scaled * n
                                store(row, level(a, b, c), image)
            return carry

        lax.fori_loop(0, FIELDS, field, 0)

    def ld(slot, row):
        return st[pl.ds(pl.multiple_of(slot * SIZE, SIZE) + row, 8), :]

    def put(slot, row, x):
        st[pl.ds(pl.multiple_of(slot * SIZE, SIZE) + row, 8), :] = x

    def tab(ref, i):
        return ref[8 * i : 8 * i + 8, :]

    def kind_0(t):
        def store(row, i, image):
            put(slot_g, row, image)
            put(work, row, tab(dh, i) * (ld(0, row) - image))

        finish(store)

    def kind_1(t):
        def store(row, i, image):
            put(work, row, tab(dh, i) * (ld(0, row) - image))

        finish(store)

    def kind_2(t):
        def store(row, i, image):
            u = tab(dh, i) * (ld(0, row) - image)
            put(first, row, u)
            put(work, row, tab(dh, i) * (u - ld(slot_g, row)))

        finish(store)

    def kind_3(t):
        def store(row, i, image):
            put(work, row, tab(dh, i) * (ld(first, row) - image))

        finish(store)

    def kind_4(t):
        def store(row, i, image):
            u1 = ld(first, row)
            u2 = tab(dh, i) * (u1 - image)
            start = ld(0, row)
            put(mid, row, u1 - 0.5 * (start + u2))
            put(work, row, (4.0 / 3.0) * u1 + (1.0 / 3.0) * u2)
            q = (5.0 / 6.0) * u2 - (2.0 / 3.0) * u1
            put(quad, row, q)
            lam = tab(el, i)
            put(base, row, lam * (2.0 * q - (1.0 / 3.0) * start) - (1.0 / 3.0) * ld(slot_g, row))

        finish(store)

    def kind_5(t):
        def store(row, i, image):
            z = ld(base, row) - image
            put(zed, row, z)
            put(work, row, 2.0 * (tab(dd, i) * (ld(0, row) + z) - ld(quad, row)))

        finish(store)

    def kind_6(t):
        def store(row, i, image):
            put(hga, row, image)
            put(c0, row, (1.0 / 3.0) * (tab(el, i) * ld(mid, row) + image))

        finish(store)

    def kind_7(t):
        def store(row, i, image):
            s = tab(dd, i) * (ld(t, row) + ld(base, row) - image)
            put(t + 1, row, s)
            put(work, row, 2.0 * (tab(dd, i) * (s + ld(zed, row)) - ld(quad, row)))

        finish(store)

    def kind_8(t):
        def store(row, i, image):
            put(slot_g + t + 1, row, image)
            s = ld(t, row)
            old = ld(slot_g + t, row)
            phi = 0.25 * (tab(el, i) * (ld(t + 1, row) - s) + image - old)
            c = ld(c0, row)
            target = s + phi + c
            put(slot_t + t, row, target)
            put(slot_p + t, row, phi - 2.0 * c)
            put(slot_v + t, row, tab(dh, i) * (target - ld(hga, row) - 0.5 * (old + image)))

        finish(store)

    def kind_9(t):
        def store(row, i, image):
            put(slot_v + t, row, tab(dh, i) * (ld(slot_t + t, row) - image))

        finish(store)

    def kind_10(t):
        def store(row, i, image):
            u = tab(dh, i) * (ld(slot_t + t, row) - image)
            put(slot_u + t, row, u)
            target = u + ld(slot_p + t, row)
            put(slot_t + t, row, target)
            put(slot_v + t, row, tab(dh, i) * (target - ld(slot_g + t + 1, row)))

        finish(store)

    def kind_11(t):
        def store(row, i, image):
            u1 = ld(slot_u + t, row)
            u2 = tab(dh, i) * (ld(slot_t + t, row) - image)
            s = ld(t, row)
            q = (5.0 / 6.0) * u2 - (2.0 / 3.0) * u1
            put(slot_p + t, row, q)
            put(slot_v + t, row, (4.0 / 3.0) * u1 + (1.0 / 3.0) * u2)
            put(slot_u + t, row, u1 - 0.5 * (s + u2))
            old = ld(slot_g + t, row)
            put(slot_t + t, row, tab(el, i) * (2.0 * q - (1.0 / 3.0) * s) - (1.0 / 3.0) * old)

        finish(store)

    def kind_12(t):
        def store(row, i, image):
            z = ld(slot_t + t, row) - image
            put(slot_v + t, row, z)
            put(work, row, 2.0 * (tab(dd, i) * (ld(0, row) + z) - ld(slot_p + t, row)))

        finish(store)

    def kind_13(t):
        later = jnp.minimum(t + 1, slices - 1)

        def store(row, i, image):
            s = tab(dd, i) * (ld(t, row) + ld(slot_t + t, row) - image)
            put(t + 1, row, s)
            z = ld(slot_v + later, row)
            put(work, row, 2.0 * (tab(dd, i) * (s + z) - ld(slot_p + later, row)))

        finish(store)

    kinds = [kind_0, kind_1, kind_2, kind_3, kind_4, kind_5, kind_6, kind_7, kind_8, kind_9]
    kinds += [kind_10, kind_11, kind_12, kind_13]

    def step(n, carry):
        transport(plan[3 * n + 1])
        faces(plan[3 * n + 1])
        lax.switch(plan[3 * n], kinds, plan[3 * n + 2])
        return carry

    lax.fori_loop(0, len(steps(slices)), step, 0)

    mine, column = where[0], where[1]
    for f in range(FIELDS):

        def own(slot):
            at = slot * SIZE + f * 256 + column
            return jnp.concatenate([st[pl.ds(at + 1280 * p, 32, 8), :] for p in (0, 1)], axis=0)

        begin, end = own(mine), own(mine + 1)
        middle = own(slot_u + mine) + 0.5 * (begin + end)
        x = jnp.concatenate([begin, middle, end], axis=1)
        r = jnp.dot(back[...], split_rows(x), preferred_element_type=f32)
        for i in range(3):
            out[i, 64 * f : 64 * f + 64, :] = r[:, 128 * i : 128 * i + 128]


def local_whole_grid(slices):
    def local(initial, viscosity, flux_jacobian):
        block = jnp.concatenate(
            [initial.reshape(ROWS, 128), jnp.broadcast_to(viscosity.reshape(1, 128), (8, 128))], axis=0
        )
        near = [block]
        for k in range(1, 4):
            near.append(lax.ppermute(block, "sy", [(i, i ^ k) for i in range(4)]))
        gathered = near + [lax.ppermute(b, "sx", [(0, 1), (1, 0)]) for b in near]

        x, y = lax.axis_index("sx"), lax.axis_index("sy")
        columns = [(x ^ (k // 4)) * 4 + (y ^ (k % 4)) for k in range(8)]
        where = jnp.stack([lax.axis_index("tm"), x * 4 + y] + columns).astype(jnp.int32)
        plan = jnp.asarray(np.array(steps(slices), np.int32).reshape(-1))

        into, back, blocks = modal_tables()
        tables = jnp.asarray(blocks, jnp.float32)
        matrix = sum(
            flux_jacobian[d][None, :, None, :, None] * tables[:, d, None, :, None, :] for d in range(3)
        ).reshape(2, 160, 160)
        matrix = jnp.concatenate([matrix, matrix, matrix], axis=2)

        smem = pl.BlockSpec(memory_space=pltpu.SMEM)
        vmem = pl.BlockSpec(memory_space=pltpu.VMEM)

        def scratch(rows):
            return pltpu.VMEM((rows, 128), jnp.float32)

        out = pl.pallas_call(
            lambda plan, where, *refs: whole_grid_kernel(slices, plan, where, *refs),
            out_shape=jax.ShapeDtypeStruct((3, ROWS, 128), jnp.float32),
            in_specs=[smem, smem] + [vmem] * 11,
            out_specs=vmem,
            scratch_shapes=[
                scratch((6 * slices + 10) * SIZE),
                scratch(SIZE),
                scratch(3840),
                pltpu.VMEM((2, 160, 480), jnp.bfloat16),
                scratch(8 * len(LEVELS)),
                scratch(8 * len(LEVELS)),
                scratch(8 * len(LEVELS)),
                scratch(8),
            ],
            compiler_params=pltpu.CompilerParams(vmem_limit_bytes=58 << 20),
        )(plan, where, *gathered, matrix, three_pass(into), three_pass(back))
        return out.reshape(1, 3, 1, 1, FIELDS, 64, 128)

    return local


def solution(mesh):
    grid = (mesh.shape["sx"], mesh.shape["sy"])
    slices = mesh.shape["tm"]
    local = local_whole_grid(slices) if grid == (2, 4) and slices <= 4 else local_exchanging
    return jax.shard_map(
        local,
        mesh=mesh,
        in_specs=(P("sx", "sy", None, None, None), P("sx", "sy", None), P()),
        out_specs=P("tm", None, "sx", "sy", None, None, None),
        check_vma=False,
    )
```

```python
import math

import jax
import jax.numpy as jnp
import numpy as np
from jax import lax
from jax.experimental import pallas as pl
from jax.experimental.pallas import tpu as pltpu
from jax.sharding import PartitionSpec as P

ITERS = 2
JF = 3
JC = 2


SIGMA = 3.0
BETA = 0.5
STEP = 0.1
HALF_STEP = 0.05
TWO_THIRDS = 2.0 / 3.0
ONE_THIRD = 1.0 / 3.0
HIGHEST = lax.Precision.HIGHEST
WEIGHTS = ((5.0 / 24.0, 1.0 / 3.0, -1.0 / 24.0), (-1.0 / 24.0, 1.0 / 3.0, 5.0 / 24.0))


def passed_along(block, axis, distance):
    devices = range(lax.axis_size(axis))
    route = [(i - distance, i) for i in devices if i - distance in devices]
    return lax.ppermute(block, axis, route)


def kron_three(first, second, third):
    return jnp.kron(jnp.kron(first, second), third)


def node_tables():
    places = jnp.arange(4)
    row = places[:, None]
    column = places[None, :]
    identity = (row == column).astype(jnp.float32)
    upper = (row + 1 == column).astype(jnp.float32)
    border = identity * ((row == 0) | (row == 3)).astype(jnp.float32)
    line_laplace = 2.0 * identity - upper - upper.T - border
    line_grad = 0.5 * upper - 0.5 * upper.T
    laplace = (
        kron_three(line_laplace, identity, identity)
        + kron_three(identity, line_laplace, identity)
        + kron_three(identity, identity, line_laplace)
        + SIGMA * jnp.eye(64, dtype=jnp.float32)
    )
    grads = jnp.stack(
        [
            kron_three(line_grad, identity, identity),
            kron_three(identity, line_grad, identity),
            kron_three(identity, identity, line_grad),
        ]
    )
    weighting = jnp.where(row == 0, 0.5, math.sqrt(0.5)).astype(jnp.float32)
    cosine = weighting * jnp.cos(
        math.pi * row.astype(jnp.float32) * (2.0 * column.astype(jnp.float32) + 1.0) / 8.0
    )
    basis = kron_three(cosine, cosine, cosine)
    line_eigen = 2.0 - 2.0 * jnp.cos(math.pi * places.astype(jnp.float32) / 4.0)
    spectrum = (
        line_eigen[:, None, None] + line_eigen[None, :, None] + line_eigen[None, None, :]
    ).reshape(64) + SIGMA
    return (laplace, grads, basis, spectrum)


def previous(array, axis):
    widths = [(0, 0)] * array.ndim
    widths[axis] = (1, 0)
    return lax.slice_in_dim(jnp.pad(array, widths), 0, array.shape[axis], axis=axis)


def following(array, axis):
    widths = [(0, 0)] * array.ndim
    widths[axis] = (0, 1)
    return lax.slice_in_dim(jnp.pad(array, widths), 1, array.shape[axis] + 1, axis=axis)


def place(before, after, axis):
    empty = jnp.zeros_like(before)
    return jnp.stack([before, empty, empty, after], axis=axis)


def neighbours(field):
    lattice = field.reshape(field.shape[:4] + (4, 4, 4) + field.shape[-1:])
    high_x = lattice[:, :, :, :, 3]
    low_x = lattice[:, :, :, :, 0]
    from_west = passed_along(high_x[:, -1], "sx", 1)
    from_east = passed_along(low_x[:, 0], "sx", -1)
    before_x = jnp.concatenate([from_west[:, None], high_x[:, :-1]], axis=1)
    after_x = jnp.concatenate([low_x[:, 1:], from_east[:, None]], axis=1)
    high_y = lattice[:, :, :, :, :, 3]
    low_y = lattice[:, :, :, :, :, 0]
    from_south = passed_along(high_y[:, :, -1], "sy", 1)
    from_north = passed_along(low_y[:, :, 0], "sy", -1)
    before_y = jnp.concatenate([from_south[:, :, None], high_y[:, :, :-1]], axis=2)
    after_y = jnp.concatenate([low_y[:, :, 1:], from_north[:, :, None]], axis=2)
    along_x = place(before_x, after_x, 4)
    along_y = place(before_y, after_y, 5)
    along_z = place(previous(lattice[..., 3, :], 6), following(lattice[..., 0, :], 6), 6)
    return (along_x + along_y + along_z).reshape(field.shape)


def apply_operator(field, coeff, flux_jacobian, laplace, grads, coupled):
    volume = jnp.einsum("mn,bxyfnz->bxyfmz", laplace, field, precision=HIGHEST)
    slopes = jnp.einsum("dmn,bxyfnz->dbxyfmz", grads, field, precision=HIGHEST)
    transport = jnp.einsum("dgf,dbxyfmz->bxygmz", flux_jacobian, slopes, precision=HIGHEST)
    return coeff * (volume - BETA * coupled) + transport


def precondition(residue, coeff, basis, spectrum, step):
    inverse = 1.0 / (1.0 + step * coeff * spectrum[:, None])
    modes = jnp.einsum("kn,bxyfnz->bxyfkz", basis, residue, precision=HIGHEST)
    return jnp.einsum("kn,bxyfkz->bxyfnz", basis, modes * inverse, precision=HIGHEST)


def block_jacobi(target, begin, force, step, turns, operate, solve):
    field = begin
    image = -force
    for turn in range(turns):
        if turn > 0:
            image = operate(field)
        field = field + solve(target - field - step * image, step)
    return field


def local_exchanging(initial, viscosity, flux_jacobian):
    laplace, grads, basis, spectrum = node_tables()
    coeff = viscosity[None, :, :, None, None, :]
    first_slice = lax.axis_index("tm") == 0

    def operate(field):
        return apply_operator(field, coeff, flux_jacobian, laplace, grads, neighbours(field))

    def solve(residue, step):
        return precondition(residue, coeff, basis, spectrum, step)

    start = initial[None]
    force_zero = -operate(start)
    values = [start, start, start]
    forces = [force_zero, force_zero, force_zero]
    for sweep in range(ITERS):
        old = list(forces)
        for node in range(2):
            weight = WEIGHTS[node]
            integral = STEP * (weight[0] * old[0] + weight[1] * old[1] + weight[2] * old[2])
            target = values[node] - HALF_STEP * old[node + 1] + integral
            values[node + 1] = block_jacobi(
                target, values[node + 1], old[node + 1], HALF_STEP, JF, operate, solve
            )
            forces[node + 1] = -operate(values[node + 1])
        correction = STEP * (TWO_THIRDS * forces[1] - ONE_THIRD * forces[0] - ONE_THIRD * forces[2])
        offset = -STEP * forces[2] + HALF_STEP * (forces[0] + forces[2]) + correction
        end_value = values[2]
        end_force = forces[2]

        def chain_turn(turn, carry):
            coarse_start, coarse_end = carry
            coarse_end = block_jacobi(
                coarse_start + offset, end_value, end_force, STEP, JC, operate, solve
            )
            passed = passed_along(coarse_end, "tm", 1)
            return (jnp.where(first_slice, start, passed), coarse_end)

        coarse_start, coarse_end = lax.fori_loop(0, lax.axis_size("tm"), chain_turn, (start, start))
        if sweep + 1 < ITERS:
            both = -operate(jnp.concatenate([coarse_start, coarse_end], axis=0))
            force_start = both[:1]
            force_end = both[1:]
            delta_start = force_start - forces[0]
            delta_end = force_end - forces[2]
            forces = [
                forces[0] + delta_start,
                forces[1] + 0.5 * (delta_start + delta_end),
                forces[2] + delta_end,
            ]
        move_start = coarse_start - values[0]
        move_end = coarse_end - values[2]
        values = [
            values[0] + move_start,
            values[1] + 0.5 * (move_start + move_end),
            values[2] + move_end,
        ]
    return jnp.stack(values, axis=1)


FIELDS = 5
ROWS = 320
SIZE = 2560
FACE = np.array([0.5] + [math.sqrt(0.5) * math.cos(math.pi * k / 8.0) for k in (1, 2, 3)])
PICK_1 = 4.0 * FACE[1] ** 2
PICK_3 = 4.0 * FACE[3] ** 2
MODES = [
    (a, b, c)
    for parity in (0, 1)
    for a in range(4)
    for b in range(4)
    for c in range(4)
    if (a + b + c) % 2 == parity
]
PLACE = {mode: (i // 32) * 160 + i % 32 for i, mode in enumerate(MODES)}
LEVELS = sorted({tuple(sorted(mode)) for mode in MODES})


def level(a, b, c):
    return LEVELS.index(tuple(sorted((a, b, c))))


def eigen(levels):
    line = [2.0 - 2.0 * math.cos(math.pi * k / 4.0) for k in range(4)]
    return sum(line[k] for k in levels) + SIGMA


def modal_tables():
    j = np.arange(4)
    cosine = np.cos(math.pi * j[:, None] * (2.0 * j[None, :] + 1.0) / 8.0)
    cosine *= np.where(j == 0, 0.5, math.sqrt(0.5))[:, None]
    basis = np.kron(np.kron(cosine, cosine), cosine)
    scale = np.kron(np.kron(FACE, FACE), FACE)
    order = [16 * a + 4 * b + c for a, b, c in MODES]
    into = (basis / scale[:, None])[order]
    back = (basis * scale[:, None])[order].T
    upper = np.eye(4, k=1)
    slope = 0.5 * upper - 0.5 * upper.T
    one = np.eye(4)
    grads = [
        np.kron(np.kron(slope, one), one),
        np.kron(np.kron(one, slope), one),
        np.kron(np.kron(one, one), slope),
    ]
    modal = np.stack([into @ grad @ back for grad in grads])
    blocks = np.stack([modal[:, 32:, :32], modal[:, :32, 32:]])
    return into, back, HALF_STEP * blocks


def three_pass(matrix):
    high = matrix.astype(jnp.bfloat16)
    low = (matrix - high.astype(np.float64)).astype(jnp.bfloat16)
    return jnp.asarray(np.concatenate([high, low, high], axis=1))


def split_rows(x):
    high = x.astype(jnp.bfloat16)
    low = (x - high.astype(jnp.float32)).astype(jnp.bfloat16)
    return jnp.concatenate([high, high, low], axis=0)


def steps(slices):
    work, mid, copy = slices, slices + 1, slices + 2
    plan = [(0, work, 0), (1, work, 0), (2, work, 0), (3, work, 0), (4, work, 0), (5, work, 0)]
    plan += [(6, mid, 0)]
    for t in range(slices):
        plan += [(7, work, t), (8, copy, t)]
    for kind in (9, 10, 9, 11):
        plan += [(kind, t, t) for t in range(slices)]
    plan += [(12, t, t) for t in reversed(range(slices))]
    plan += [(13, work, t) for t in range(slices)]
    return plan


def whole_grid_kernel(slices, plan, where, *refs):
    gathered, refs = refs[:8], refs[8:]
    matrix, into, back, out, *refs = refs
    ss, gg, tt, pp, vv, uu, first, quad, base, zed, c0, hga, tr, g, m, dh, dd, el, cc = refs
    f32 = jnp.float32
    work, mid, copy = slices * SIZE, (slices + 1) * SIZE, (slices + 2) * SIZE

    for k in range(8):
        cc[pl.ds(where[2 + k], 1), :] = gathered[k][320:321, :]
    visc = cc[...]
    for i, levels in enumerate(LEVELS):
        lam = (HALF_STEP * eigen(levels)) * visc
        el[8 * i : 8 * i + 8, :] = lam
        dh[8 * i : 8 * i + 8, :] = 1.0 / (1.0 + lam)
        dd[8 * i : 8 * i + 8, :] = 1.0 / (1.0 + 2.0 * lam)
    for p in range(2):
        whole = matrix[p]
        high = whole.astype(jnp.bfloat16).astype(f32)
        lane = lax.broadcasted_iota(jnp.int32, whole.shape, 1)
        middle = (lane >= 160) & (lane < 320)
        m[p] = jnp.where(middle, whole - high, high).astype(jnp.bfloat16)
    for k in range(0, 8, 2):
        for f in range(FIELDS):
            x = jnp.concatenate([gathered[k + i][64 * f : 64 * f + 64, :] for i in (0, 1)], axis=1)
            r = jnp.dot(into[...], split_rows(x), preferred_element_type=f32)
            for i in (0, 1):
                for p in (0, 1):
                    at = p * 1280 + f * 256 + where[2 + k + i]
                    part = r[32 * p : 32 * p + 32, 128 * i : 128 * i + 128]
                    ss[pl.ds(at, 32, 8), :] = part
                    vv[pl.ds(work + at, 32, 8), :] = part

    sub = lax.broadcasted_iota(jnp.int32, (8, 128), 0)
    lane = lax.broadcasted_iota(jnp.int32, (8, 128), 1)
    tau = jnp.where(sub >= 4, 1.0, -1.0).astype(f32)
    y_first, y_last = sub % 4 == 0, sub % 4 == 3
    z_first, z_last = lane == 0, lane == 127
    scaled = (HALF_STEP * BETA * 0.25) * visc

    def transport(at):
        for jp in range(4):
            for p in range(2):
                begin = at + (p * 1280 + 2 * jp)
                x = jnp.concatenate([vv[pl.ds(begin + i, 160, 8), :] for i in (0, 1)], axis=1)
                r = jnp.dot(m[p], split_rows(x), preferred_element_type=f32)
                for i in (0, 1):
                    tr[pl.ds((1 - p) * 1280 + 2 * jp + i, 160, 8), :] = r[:, 128 * i : 128 * i + 128]
            yield

    def faces(at_x, at_y, at_z):
        def ld(at, a, b, c):
            return vv[pl.ds(at + (256 * f + 8 * PLACE[a, b, c]), 8), :]

        for f in range(FIELDS):
            for p in range(4):
                for q in range(4):
                    i = 8 * (16 * f + 4 * p + q)
                    even = ld(at_x, 0, p, q) + ld(at_x, 2, p, q)
                    odd = PICK_1 * ld(at_x, 1, p, q) + PICK_3 * ld(at_x, 3, p, q)
                    met = pltpu.roll(even + tau * odd, 4, 0)
                    g[i : i + 8, :] = met
                    g[640 + i : 648 + i, :] = tau * met
                    even = ld(at_y, p, 0, q) + ld(at_y, p, 2, q)
                    odd = PICK_1 * ld(at_y, p, 1, q) + PICK_3 * ld(at_y, p, 3, q)
                    low = jnp.where(y_first, 0.0, pltpu.roll(even - odd, 1, 0))
                    high = jnp.where(y_last, 0.0, pltpu.roll(even + odd, 7, 0))
                    g[1280 + i : 1288 + i, :] = low + high
                    g[1920 + i : 1928 + i, :] = low - high
                    even = ld(at_z, p, q, 0) + ld(at_z, p, q, 2)
                    odd = PICK_1 * ld(at_z, p, q, 1) + PICK_3 * ld(at_z, p, q, 3)
                    low = jnp.where(z_first, 0.0, pltpu.roll(even - odd, 1, 1))
                    high = jnp.where(z_last, 0.0, pltpu.roll(even + odd, 127, 1))
                    g[2560 + i : 2568 + i, :] = low + high
                    g[3200 + i : 3208 + i, :] = low - high
            yield

    def finish(store):
        def field(f, carry):
            at = pl.multiple_of(f * 256, 256)
            gat = pl.multiple_of(f * 128, 128)
            for pa in range(2):
                for pb in range(2):
                    gx = {
                        (b, c): g[pl.ds(gat + (640 * pa + 8 * (4 * b + c)), 8), :]
                        for b in (pb, pb + 2)
                        for c in range(4)
                    }
                    gy = {
                        (a, c): g[pl.ds(gat + (1280 + 640 * pb + 8 * (4 * a + c)), 8), :]
                        for a in (pa, pa + 2)
                        for c in range(4)
                    }
                    for a in (pa, pa + 2):
                        for b in (pb, pb + 2):
                            gz = [
                                g[pl.ds(gat + (2560 + 640 * pc + 8 * (4 * a + b)), 8), :]
                                for pc in range(2)
                            ]
                            for c in range(4):
                                row = 8 * PLACE[a, b, c]
                                n = gx[b, c] + gy[a, c] + gz[c % 2]
                                image = tr[pl.ds(at + row, 8), :] - scaled * n
                                store((at, row), level(a, b, c), image)
            return carry

        lax.fori_loop(0, FIELDS, field, 0)

    def ld(ref, row, start=0, more=0):
        return ref[pl.ds(pl.multiple_of(start + row[0], 256) + (more + row[1]), 8), :]

    def put(ref, row, x, start=0, more=0):
        ref[pl.ds(pl.multiple_of(start + row[0], 256) + (more + row[1]), 8), :] = x

    def tab(ref, i):
        return ref[8 * i : 8 * i + 8, :]

    def kind_0(t):
        def store(row, i, image):
            put(gg, row, image)
            put(vv, row, tab(dh, i) * (ld(ss, row) - image), 0, work)

        finish(store)

    def kind_1(t):
        def store(row, i, image):
            put(vv, row, tab(dh, i) * (ld(ss, row) - image), 0, work)

        finish(store)

    def kind_2(t):
        def store(row, i, image):
            u = tab(dh, i) * (ld(ss, row) - image)
            put(first, row, u)
            put(vv, row, tab(dh, i) * (u - ld(gg, row)), 0, work)

        finish(store)

    def kind_3(t):
        def store(row, i, image):
            put(vv, row, tab(dh, i) * (ld(first, row) - image), 0, work)

        finish(store)

    def kind_4(t):
        def store(row, i, image):
            u1 = ld(first, row)
            u2 = tab(dh, i) * (u1 - image)
            start = ld(ss, row)
            put(vv, row, u1 - 0.5 * (start + u2), 0, mid)
            put(vv, row, (4.0 / 3.0) * u1 + (1.0 / 3.0) * u2, 0, work)
            q = (5.0 / 6.0) * u2 - (2.0 / 3.0) * u1
            put(quad, row, q)
            lam = tab(el, i)
            put(base, row, lam * (2.0 * q - (1.0 / 3.0) * start) - (1.0 / 3.0) * ld(gg, row))

        finish(store)

    def kind_5(t):
        def store(row, i, image):
            z = ld(base, row) - image
            put(zed, row, z)
            put(vv, row, 2.0 * (tab(dd, i) * (ld(ss, row) + z) - ld(quad, row)), 0, work)

        finish(store)

    def kind_6(t):
        def store(row, i, image):
            put(hga, row, image)
            put(c0, row, (1.0 / 3.0) * (tab(el, i) * ld(vv, row, 0, mid) + image))

        finish(store)

    def kind_7(t):
        at = t * SIZE

        def store(row, i, image):
            s = tab(dd, i) * (ld(ss, row, at) + ld(base, row) - image)
            put(ss, row, s, at, SIZE)
            put(vv, row, s, 0, copy)
            put(vv, row, 2.0 * (tab(dd, i) * (s + ld(zed, row)) - ld(quad, row)), 0, work)

        finish(store)

    def kind_8(t):
        at = t * SIZE

        def store(row, i, image):
            put(gg, row, image, at, SIZE)
            s = ld(ss, row, at)
            old = ld(gg, row, at)
            phi = 0.25 * (tab(el, i) * (ld(ss, row, at, SIZE) - s) + image - old)
            c = ld(c0, row)
            target = s + phi + c
            put(tt, row, target, at)
            put(pp, row, phi - 2.0 * c, at)
            put(vv, row, tab(dh, i) * (target - ld(hga, row) - 0.5 * (old + image)), at)

        finish(store)

    def kind_9(t):
        at = t * SIZE

        def store(row, i, image):
            put(vv, row, tab(dh, i) * (ld(tt, row, at) - image), at)

        finish(store)

    def kind_10(t):
        at = t * SIZE

        def store(row, i, image):
            u = tab(dh, i) * (ld(tt, row, at) - image)
            put(uu, row, u, at)
            target = u + ld(pp, row, at)
            put(tt, row, target, at)
            put(vv, row, tab(dh, i) * (target - ld(gg, row, at, SIZE)), at)

        finish(store)

    def kind_11(t):
        at = t * SIZE

        def store(row, i, image):
            u1 = ld(uu, row, at)
            u2 = tab(dh, i) * (ld(tt, row, at) - image)
            s = ld(ss, row, at)
            q = (5.0 / 6.0) * u2 - (2.0 / 3.0) * u1
            put(pp, row, q, at)
            put(vv, row, (4.0 / 3.0) * u1 + (1.0 / 3.0) * u2, at)
            put(uu, row, u1 - 0.5 * (s + u2), at)
            old = ld(gg, row, at)
            put(tt, row, tab(el, i) * (2.0 * q - (1.0 / 3.0) * s) - (1.0 / 3.0) * old, at)

        finish(store)

    def kind_12(t):
        at = t * SIZE

        def store(row, i, image):
            z = ld(tt, row, at) - image
            put(gg, row, z, at)
            put(vv, row, 2.0 * (tab(dd, i) * (ld(ss, row) + z) - ld(pp, row, at)), 0, work)

        finish(store)

    def kind_13(t):
        at = t * SIZE
        later = jnp.minimum(t + 1, slices - 1) * SIZE

        def store(row, i, image):
            s = tab(dd, i) * (ld(ss, row, at) + ld(tt, row, at) - image)
            put(ss, row, s, at, SIZE)
            z = ld(gg, row, later)
            put(vv, row, 2.0 * (tab(dd, i) * (s + z) - ld(pp, row, later)), 0, work)

        finish(store)

    kinds = [kind_0, kind_1, kind_2, kind_3, kind_4, kind_5, kind_6, kind_7, kind_8, kind_9]
    kinds += [kind_10, kind_11, kind_12, kind_13]

    def step(n, carry):
        at = [pl.multiple_of(plan[5 * n + i], SIZE) for i in range(1, 4)]
        one, other = transport(at[0]), faces(*at)
        for _ in other:
            next(one, None)
        lax.switch(plan[5 * n], kinds, plan[5 * n + 4])
        return carry

    lax.fori_loop(0, len(steps(slices)), step, 0)

    mine, column = where[0], where[1]
    for f in range(FIELDS):

        def own(ref, slot):
            at = slot * SIZE + f * 256 + column
            return jnp.concatenate([ref[pl.ds(at + 1280 * p, 32, 8), :] for p in (0, 1)], axis=0)

        begin, end = own(ss, mine), own(ss, mine + 1)
        middle = own(uu, mine) + 0.5 * (begin + end)
        x = jnp.concatenate([begin, middle, end], axis=1)
        r = jnp.dot(back[...], split_rows(x), preferred_element_type=f32)
        for i in range(3):
            out[i, 64 * f : 64 * f + 64, :] = r[:, 128 * i : 128 * i + 128]


def local_whole_grid(slices):
    def local(initial, viscosity, flux_jacobian):
        block = jnp.concatenate(
            [initial.reshape(ROWS, 128), jnp.broadcast_to(viscosity.reshape(1, 128), (8, 128))], axis=0
        )
        near = [block]
        for k in range(1, 4):
            near.append(lax.ppermute(block, "sy", [(i, i ^ k) for i in range(4)]))
        gathered = near + [lax.ppermute(b, "sx", [(0, 1), (1, 0)]) for b in near]

        x, y = lax.axis_index("sx"), lax.axis_index("sy")
        columns = [(x ^ (k // 4)) * 4 + (y ^ (k % 4)) for k in range(8)]
        where = jnp.stack([lax.axis_index("tm"), x * 4 + y] + columns).astype(jnp.int32)
        plan = [(kind, at * SIZE, at * SIZE, at * SIZE, t) for kind, at, t in steps(slices)]
        plan = jnp.asarray(np.array(plan, np.int32).reshape(-1))

        into, back, blocks = modal_tables()
        tables = jnp.asarray(blocks, jnp.float32)
        matrix = sum(
            flux_jacobian[d][None, :, None, :, None] * tables[:, d, None, :, None, :] for d in range(3)
        ).reshape(2, 160, 160)
        matrix = jnp.concatenate([matrix, matrix, matrix], axis=2)

        smem = pl.BlockSpec(memory_space=pltpu.SMEM)
        vmem = pl.BlockSpec(memory_space=pltpu.VMEM)

        def scratch(rows):
            return pltpu.VMEM((rows, 128), jnp.float32)

        out = pl.pallas_call(
            lambda plan, where, *refs: whole_grid_kernel(slices, plan, where, *refs),
            out_shape=jax.ShapeDtypeStruct((3, ROWS, 128), jnp.float32),
            in_specs=[smem, smem] + [vmem] * 11,
            out_specs=vmem,
            scratch_shapes=[
                scratch((slices + 1) * SIZE),
                scratch((slices + 1) * SIZE),
                scratch(slices * SIZE),
                scratch(slices * SIZE),
                scratch((slices + 3) * SIZE),
                scratch(slices * SIZE),
                *[scratch(SIZE)] * 6,
                scratch(SIZE),
                scratch(3840),
                pltpu.VMEM((2, 160, 480), jnp.bfloat16),
                scratch(8 * len(LEVELS)),
                scratch(8 * len(LEVELS)),
                scratch(8 * len(LEVELS)),
                scratch(8),
            ],
            compiler_params=pltpu.CompilerParams(vmem_limit_bytes=58 << 20),
        )(plan, where, *gathered, matrix, three_pass(into), three_pass(back))
        return out.reshape(1, 3, 1, 1, FIELDS, 64, 128)

    return local


def solution(mesh):
    grid = (mesh.shape["sx"], mesh.shape["sy"])
    slices = mesh.shape["tm"]
    local = local_whole_grid(slices) if grid == (2, 4) and slices <= 4 else local_exchanging
    return jax.shard_map(
        local,
        mesh=mesh,
        in_specs=(P("sx", "sy", None, None, None), P("sx", "sy", None), P()),
        out_specs=P("tm", None, "sx", "sy", None, None, None),
        check_vma=False,
    )
```

```python
import math

import jax
import jax.numpy as jnp
import numpy as np
from jax import lax
from jax.experimental import pallas as pl
from jax.experimental.pallas import tpu as pltpu
from jax.sharding import PartitionSpec as P

ITERS = 2
JF = 3
JC = 2


SIGMA = 3.0
BETA = 0.5
STEP = 0.1
HALF_STEP = 0.05
TWO_THIRDS = 2.0 / 3.0
ONE_THIRD = 1.0 / 3.0
HIGHEST = lax.Precision.HIGHEST
WEIGHTS = ((5.0 / 24.0, 1.0 / 3.0, -1.0 / 24.0), (-1.0 / 24.0, 1.0 / 3.0, 5.0 / 24.0))


def passed_along(block, axis, distance):
    devices = range(lax.axis_size(axis))
    route = [(i - distance, i) for i in devices if i - distance in devices]
    return lax.ppermute(block, axis, route)


def kron_three(first, second, third):
    return jnp.kron(jnp.kron(first, second), third)


def node_tables():
    places = jnp.arange(4)
    row = places[:, None]
    column = places[None, :]
    identity = (row == column).astype(jnp.float32)
    upper = (row + 1 == column).astype(jnp.float32)
    border = identity * ((row == 0) | (row == 3)).astype(jnp.float32)
    line_laplace = 2.0 * identity - upper - upper.T - border
    line_grad = 0.5 * upper - 0.5 * upper.T
    laplace = (
        kron_three(line_laplace, identity, identity)
        + kron_three(identity, line_laplace, identity)
        + kron_three(identity, identity, line_laplace)
        + SIGMA * jnp.eye(64, dtype=jnp.float32)
    )
    grads = jnp.stack(
        [
            kron_three(line_grad, identity, identity),
            kron_three(identity, line_grad, identity),
            kron_three(identity, identity, line_grad),
        ]
    )
    weighting = jnp.where(row == 0, 0.5, math.sqrt(0.5)).astype(jnp.float32)
    cosine = weighting * jnp.cos(
        math.pi * row.astype(jnp.float32) * (2.0 * column.astype(jnp.float32) + 1.0) / 8.0
    )
    basis = kron_three(cosine, cosine, cosine)
    line_eigen = 2.0 - 2.0 * jnp.cos(math.pi * places.astype(jnp.float32) / 4.0)
    spectrum = (
        line_eigen[:, None, None] + line_eigen[None, :, None] + line_eigen[None, None, :]
    ).reshape(64) + SIGMA
    return (laplace, grads, basis, spectrum)


def previous(array, axis):
    widths = [(0, 0)] * array.ndim
    widths[axis] = (1, 0)
    return lax.slice_in_dim(jnp.pad(array, widths), 0, array.shape[axis], axis=axis)


def following(array, axis):
    widths = [(0, 0)] * array.ndim
    widths[axis] = (0, 1)
    return lax.slice_in_dim(jnp.pad(array, widths), 1, array.shape[axis] + 1, axis=axis)


def place(before, after, axis):
    empty = jnp.zeros_like(before)
    return jnp.stack([before, empty, empty, after], axis=axis)


def neighbours(field):
    lattice = field.reshape(field.shape[:4] + (4, 4, 4) + field.shape[-1:])
    high_x = lattice[:, :, :, :, 3]
    low_x = lattice[:, :, :, :, 0]
    from_west = passed_along(high_x[:, -1], "sx", 1)
    from_east = passed_along(low_x[:, 0], "sx", -1)
    before_x = jnp.concatenate([from_west[:, None], high_x[:, :-1]], axis=1)
    after_x = jnp.concatenate([low_x[:, 1:], from_east[:, None]], axis=1)
    high_y = lattice[:, :, :, :, :, 3]
    low_y = lattice[:, :, :, :, :, 0]
    from_south = passed_along(high_y[:, :, -1], "sy", 1)
    from_north = passed_along(low_y[:, :, 0], "sy", -1)
    before_y = jnp.concatenate([from_south[:, :, None], high_y[:, :, :-1]], axis=2)
    after_y = jnp.concatenate([low_y[:, :, 1:], from_north[:, :, None]], axis=2)
    along_x = place(before_x, after_x, 4)
    along_y = place(before_y, after_y, 5)
    along_z = place(previous(lattice[..., 3, :], 6), following(lattice[..., 0, :], 6), 6)
    return (along_x + along_y + along_z).reshape(field.shape)


def apply_operator(field, coeff, flux_jacobian, laplace, grads, coupled):
    volume = jnp.einsum("mn,bxyfnz->bxyfmz", laplace, field, precision=HIGHEST)
    slopes = jnp.einsum("dmn,bxyfnz->dbxyfmz", grads, field, precision=HIGHEST)
    transport = jnp.einsum("dgf,dbxyfmz->bxygmz", flux_jacobian, slopes, precision=HIGHEST)
    return coeff * (volume - BETA * coupled) + transport


def precondition(residue, coeff, basis, spectrum, step):
    inverse = 1.0 / (1.0 + step * coeff * spectrum[:, None])
    modes = jnp.einsum("kn,bxyfnz->bxyfkz", basis, residue, precision=HIGHEST)
    return jnp.einsum("kn,bxyfkz->bxyfnz", basis, modes * inverse, precision=HIGHEST)


def block_jacobi(target, begin, force, step, turns, operate, solve):
    field = begin
    image = -force
    for turn in range(turns):
        if turn > 0:
            image = operate(field)
        field = field + solve(target - field - step * image, step)
    return field


def local_exchanging(initial, viscosity, flux_jacobian):
    laplace, grads, basis, spectrum = node_tables()
    coeff = viscosity[None, :, :, None, None, :]
    first_slice = lax.axis_index("tm") == 0

    def operate(field):
        return apply_operator(field, coeff, flux_jacobian, laplace, grads, neighbours(field))

    def solve(residue, step):
        return precondition(residue, coeff, basis, spectrum, step)

    start = initial[None]
    force_zero = -operate(start)
    values = [start, start, start]
    forces = [force_zero, force_zero, force_zero]
    for sweep in range(ITERS):
        old = list(forces)
        for node in range(2):
            weight = WEIGHTS[node]
            integral = STEP * (weight[0] * old[0] + weight[1] * old[1] + weight[2] * old[2])
            target = values[node] - HALF_STEP * old[node + 1] + integral
            values[node + 1] = block_jacobi(
                target, values[node + 1], old[node + 1], HALF_STEP, JF, operate, solve
            )
            forces[node + 1] = -operate(values[node + 1])
        correction = STEP * (TWO_THIRDS * forces[1] - ONE_THIRD * forces[0] - ONE_THIRD * forces[2])
        offset = -STEP * forces[2] + HALF_STEP * (forces[0] + forces[2]) + correction
        end_value = values[2]
        end_force = forces[2]

        def chain_turn(turn, carry):
            coarse_start, coarse_end = carry
            coarse_end = block_jacobi(
                coarse_start + offset, end_value, end_force, STEP, JC, operate, solve
            )
            passed = passed_along(coarse_end, "tm", 1)
            return (jnp.where(first_slice, start, passed), coarse_end)

        coarse_start, coarse_end = lax.fori_loop(0, lax.axis_size("tm"), chain_turn, (start, start))
        if sweep + 1 < ITERS:
            both = -operate(jnp.concatenate([coarse_start, coarse_end], axis=0))
            force_start = both[:1]
            force_end = both[1:]
            delta_start = force_start - forces[0]
            delta_end = force_end - forces[2]
            forces = [
                forces[0] + delta_start,
                forces[1] + 0.5 * (delta_start + delta_end),
                forces[2] + delta_end,
            ]
        move_start = coarse_start - values[0]
        move_end = coarse_end - values[2]
        values = [
            values[0] + move_start,
            values[1] + 0.5 * (move_start + move_end),
            values[2] + move_end,
        ]
    return jnp.stack(values, axis=1)


FIELDS = 5
ROWS = 320
SIZE = 2560
FACE = np.array([0.5] + [math.sqrt(0.5) * math.cos(math.pi * k / 8.0) for k in (1, 2, 3)])
PICK_1 = 4.0 * FACE[1] ** 2
PICK_3 = 4.0 * FACE[3] ** 2
MODES = [
    (a, b, c)
    for parity in (0, 1)
    for a in range(4)
    for b in range(4)
    for c in range(4)
    if (a + b + c) % 2 == parity
]
PLACE = {mode: (i // 32) * 160 + i % 32 for i, mode in enumerate(MODES)}
LEVELS = sorted({tuple(sorted(mode)) for mode in MODES})


def level(a, b, c):
    return LEVELS.index(tuple(sorted((a, b, c))))


def eigen(levels):
    line = [2.0 - 2.0 * math.cos(math.pi * k / 4.0) for k in range(4)]
    return sum(line[k] for k in levels) + SIGMA


def modal_tables():
    j = np.arange(4)
    cosine = np.cos(math.pi * j[:, None] * (2.0 * j[None, :] + 1.0) / 8.0)
    cosine *= np.where(j == 0, 0.5, math.sqrt(0.5))[:, None]
    basis = np.kron(np.kron(cosine, cosine), cosine)
    scale = np.kron(np.kron(FACE, FACE), FACE)
    order = [16 * a + 4 * b + c for a, b, c in MODES]
    into = (basis / scale[:, None])[order]
    back = (basis * scale[:, None])[order].T
    upper = np.eye(4, k=1)
    slope = 0.5 * upper - 0.5 * upper.T
    one = np.eye(4)
    grads = [
        np.kron(np.kron(slope, one), one),
        np.kron(np.kron(one, slope), one),
        np.kron(np.kron(one, one), slope),
    ]
    modal = np.stack([into @ grad @ back for grad in grads])
    blocks = np.stack([modal[:, 32:, :32], modal[:, :32, 32:]])
    return into, back, HALF_STEP * blocks


def three_pass(matrix):
    high = matrix.astype(jnp.bfloat16)
    low = (matrix - high.astype(np.float64)).astype(jnp.bfloat16)
    return jnp.asarray(np.concatenate([high, low, high], axis=1))


def split_rows(x):
    high = x.astype(jnp.bfloat16)
    low = (x - high.astype(jnp.float32)).astype(jnp.bfloat16)
    return jnp.concatenate([high, high, low], axis=0)


ORDER = [9, 8, 7, 10, 11, 12, 13, 0, 1, 2, 3, 4, 5, 6]


def steps(slices):
    work, mid, copy = slices, slices + 1, slices + 2
    plan = [(0, work, 0), (1, work, 0), (2, work, 0), (3, work, 0), (4, work, 0), (5, work, 0)]
    plan += [(6, mid, 0)]
    for t in range(slices):
        plan += [(7, work, t), (8, copy, t)]
    for kind in (9, 10, 9, 11):
        plan += [(kind, t, t) for t in range(slices)]
    plan += [(12, t, t) for t in reversed(range(slices))]
    plan += [(13, work, t) for t in range(slices)]
    return plan


def whole_grid_kernel(slices, plan, *refs):
    gathered, refs = refs[:8], refs[8:]
    matrix, into, back, out, *refs = refs
    ss, gg, tt, pp, vv, uu, first, quad, base, zed, c0, hga, c2, tr, g, m, dh, dd, de, el, cc, gin, sems = refs
    f32 = jnp.float32
    work, mid, copy = slices * SIZE, (slices + 1) * SIZE, (slices + 2) * SIZE

    copies = [pltpu.make_async_copy(gathered[k], gin.at[k], sems.at[k]) for k in range(8)]
    for copy_in in copies:
        copy_in.start()
    x_here, y_here = lax.axis_index("sx"), lax.axis_index("sy")
    mine, column = lax.axis_index("tm"), 4 * x_here + y_here
    places = [(x_here ^ (k // 4)) * 4 + (y_here ^ (k % 4)) for k in range(8)]
    for p in range(2):
        whole = matrix[p]
        high = whole.astype(jnp.bfloat16).astype(f32)
        m[p] = jnp.concatenate([high, whole - high, high], axis=1).astype(jnp.bfloat16)
    for copy_in in copies:
        copy_in.wait()
    for k in range(8):
        cc[pl.ds(places[k], 1), :] = gin[k, 320:321, :]
    visc = cc[...]
    for i, levels in enumerate(LEVELS):
        lam = (HALF_STEP * eigen(levels)) * visc
        el[8 * i : 8 * i + 8, :] = lam
        dh[8 * i : 8 * i + 8, :] = 1.0 / (1.0 + lam)
        dd[8 * i : 8 * i + 8, :] = 1.0 / (1.0 + 2.0 * lam)
        de[8 * i : 8 * i + 8, :] = 2.0 / (1.0 + 2.0 * lam)
    for k in range(0, 8, 2):
        for f in range(FIELDS):
            x = jnp.concatenate([gin[k + i, 64 * f : 64 * f + 64, :] for i in (0, 1)], axis=1)
            r = jnp.dot(into[...], split_rows(x), preferred_element_type=f32)
            for i in (0, 1):
                for p in (0, 1):
                    at = p * 1280 + f * 256 + places[k + i]
                    part = r[32 * p : 32 * p + 32, 128 * i : 128 * i + 128]
                    ss[pl.ds(at, 32, 8), :] = part
                    vv[pl.ds(work + at, 32, 8), :] = part

    sub = lax.broadcasted_iota(jnp.int32, (8, 128), 0)
    lane = lax.broadcasted_iota(jnp.int32, (8, 128), 1)
    tau = jnp.where(sub >= 4, 1.0, -1.0).astype(f32)
    tau_1, tau_3 = PICK_1 * tau, PICK_3 * tau
    y_first, y_last = sub % 4 == 0, sub % 4 == 3
    z_first, z_last = lane == 0, lane == 127
    scaled = (HALF_STEP * BETA * 0.25) * visc

    def transport(at):
        for half in range(2):
            for p in range(2):
                begin = at + (p * 1280 + 4 * half)
                x = jnp.concatenate([vv[pl.ds(begin + i, 160, 8), :] for i in range(4)], axis=1)
                r = jnp.dot(m[p], split_rows(x), preferred_element_type=f32)
                for i in range(4):
                    row = (1 - p) * 1280 + 4 * half + i
                    tr[pl.ds(row, 160, 8), :] = r[:, 128 * i : 128 * i + 128]
                yield

    def faces(at_x, at_y, at_z):
        def ld(at, a, b, c):
            return vv[pl.ds(at + (256 * f + 8 * PLACE[a, b, c]), 8), :]

        for f in range(FIELDS):
            for p in range(4):
                for q in range(4):
                    i = 8 * (16 * f + 4 * p + q)
                    even = ld(at_x, 0, p, q) + ld(at_x, 2, p, q)
                    odd = tau_1 * ld(at_x, 1, p, q) + tau_3 * ld(at_x, 3, p, q)
                    met = pltpu.roll(even + odd, 4, 0)
                    g[i : i + 8, :] = met
                    g[640 + i : 648 + i, :] = tau * met
                    even = ld(at_y, p, 0, q) + ld(at_y, p, 2, q)
                    odd = PICK_1 * ld(at_y, p, 1, q) + PICK_3 * ld(at_y, p, 3, q)
                    low = jnp.where(y_first, 0.0, pltpu.roll(even - odd, 1, 0))
                    high = jnp.where(y_last, 0.0, pltpu.roll(even + odd, 7, 0))
                    g[1280 + i : 1288 + i, :] = low + high
                    g[1920 + i : 1928 + i, :] = low - high
                    even = ld(at_z, p, q, 0) + ld(at_z, p, q, 2)
                    odd = PICK_1 * ld(at_z, p, q, 1) + PICK_3 * ld(at_z, p, q, 3)
                    low = jnp.where(z_first, 0.0, pltpu.roll(even - odd, 1, 1))
                    high = jnp.where(z_last, 0.0, pltpu.roll(even + odd, 127, 1))
                    g[2560 + i : 2568 + i, :] = low + high
                    g[3200 + i : 3208 + i, :] = low - high
            yield

    def finish(store):
        def field(f, carry):
            at = pl.multiple_of(f * 256, 256)
            gat = pl.multiple_of(f * 128, 128)
            for pa in range(2):
                for pb in range(2):
                    gx = {
                        (b, c): g[pl.ds(gat + (640 * pa + 8 * (4 * b + c)), 8), :]
                        for b in (pb, pb + 2)
                        for c in range(4)
                    }
                    gy = {
                        (a, c): g[pl.ds(gat + (1280 + 640 * pb + 8 * (4 * a + c)), 8), :]
                        for a in (pa, pa + 2)
                        for c in range(4)
                    }
                    for a in (pa, pa + 2):
                        for b in (pb, pb + 2):
                            gz = [
                                g[pl.ds(gat + (2560 + 640 * pc + 8 * (4 * a + b)), 8), :]
                                for pc in range(2)
                            ]
                            for c in range(4):
                                row = 8 * PLACE[a, b, c]
                                n = gx[b, c] + gy[a, c] + gz[c % 2]
                                image = tr[pl.ds(at + row, 8), :] - scaled * n
                                store((at, row), level(a, b, c), image)
            return carry

        lax.fori_loop(0, FIELDS, field, 0)

    def ld(ref, row, start=0, more=0):
        return ref[pl.ds(pl.multiple_of(start + row[0], 256) + (more + row[1]), 8), :]

    def put(ref, row, x, start=0, more=0):
        ref[pl.ds(pl.multiple_of(start + row[0], 256) + (more + row[1]), 8), :] = x

    def tab(ref, i):
        return ref[8 * i : 8 * i + 8, :]

    def kind_0(t):
        def store(row, i, image):
            put(gg, row, image)
            put(vv, row, tab(dh, i) * (ld(ss, row) - image), 0, work)

        finish(store)

    def kind_1(t):
        def store(row, i, image):
            put(vv, row, tab(dh, i) * (ld(ss, row) - image), 0, work)

        finish(store)

    def kind_2(t):
        def store(row, i, image):
            u = tab(dh, i) * (ld(ss, row) - image)
            put(first, row, u)
            put(vv, row, tab(dh, i) * (u - ld(gg, row)), 0, work)

        finish(store)

    def kind_3(t):
        def store(row, i, image):
            put(vv, row, tab(dh, i) * (ld(first, row) - image), 0, work)

        finish(store)

    def kind_4(t):
        def store(row, i, image):
            u1 = ld(first, row)
            u2 = tab(dh, i) * (u1 - image)
            start = ld(ss, row)
            put(vv, row, u1 - 0.5 * (start + u2), 0, mid)
            mix = (4.0 / 3.0) * u1 + (1.0 / 3.0) * u2
            put(vv, row, mix, 0, work)
            q = u2 + u2 - mix
            put(quad, row, q)
            put(base, row, tab(el, i) * (q - (1.0 / 3.0) * start) - (1.0 / 3.0) * ld(gg, row))

        finish(store)

    def kind_5(t):
        def store(row, i, image):
            z = ld(base, row) - image
            put(zed, row, z)
            put(vv, row, tab(de, i) * (ld(ss, row) + z) - ld(quad, row), 0, work)

        finish(store)

    def kind_6(t):
        def store(row, i, image):
            put(hga, row, image)
            c = (1.0 / 3.0) * (tab(el, i) * ld(vv, row, 0, mid) + image)
            put(c0, row, c)
            put(c2, row, c + c)

        finish(store)

    def kind_7(t):
        at = t * SIZE

        def store(row, i, image):
            s = tab(dd, i) * (ld(ss, row, at) + ld(base, row) - image)
            put(ss, row, s, at, SIZE)
            put(vv, row, s, 0, copy)
            put(vv, row, tab(de, i) * (s + ld(zed, row)) - ld(quad, row), 0, work)

        finish(store)

    def kind_8(t):
        at = t * SIZE

        def store(row, i, image):
            put(gg, row, image, at, SIZE)
            s = ld(ss, row, at)
            old = ld(gg, row, at)
            phi = 0.25 * (tab(el, i) * (ld(ss, row, at, SIZE) - s) + image - old)
            target = s + phi + ld(c0, row)
            put(tt, row, target, at)
            put(pp, row, phi - ld(c2, row), at)
            put(vv, row, tab(dh, i) * (target - ld(hga, row) - 0.5 * (old + image)), at)

        finish(store)

    def kind_9(t):
        at = t * SIZE

        def store(row, i, image):
            put(vv, row, tab(dh, i) * (ld(tt, row, at) - image), at)

        finish(store)

    def kind_10(t):
        at = t * SIZE

        def store(row, i, image):
            u = tab(dh, i) * (ld(tt, row, at) - image)
            put(uu, row, u, at)
            target = u + ld(pp, row, at)
            put(tt, row, target, at)
            put(vv, row, tab(dh, i) * (target - ld(gg, row, at, SIZE)), at)

        finish(store)

    def kind_11(t):
        at = t * SIZE

        def store(row, i, image):
            u1 = ld(uu, row, at)
            u2 = tab(dh, i) * (ld(tt, row, at) - image)
            s = ld(ss, row, at)
            mix = (4.0 / 3.0) * u1 + (1.0 / 3.0) * u2
            put(vv, row, mix, at)
            q = u2 + u2 - mix
            put(pp, row, q, at)
            put(uu, row, u1 - 0.5 * (s + u2), at)
            old = ld(gg, row, at)
            put(tt, row, tab(el, i) * (q - (1.0 / 3.0) * s) - (1.0 / 3.0) * old, at)

        finish(store)

    def kind_12(t):
        at = t * SIZE

        def store(row, i, image):
            z = ld(tt, row, at) - image
            put(gg, row, z, at)
            put(vv, row, tab(de, i) * (ld(ss, row) + z) - ld(pp, row, at), 0, work)

        finish(store)

    def kind_13(t):
        at = t * SIZE
        later = jnp.minimum(t + 1, slices - 1) * SIZE

        def store(row, i, image):
            s = tab(dd, i) * (ld(ss, row, at) + ld(tt, row, at) - image)
            put(ss, row, s, at, SIZE)
            z = ld(gg, row, later)
            put(vv, row, tab(de, i) * (s + z) - ld(pp, row, later), 0, work)

        finish(store)

    kinds = [kind_9, kind_8, kind_7, kind_10, kind_11, kind_12, kind_13]
    kinds += [kind_0, kind_1, kind_2, kind_3, kind_4, kind_5, kind_6]

    def step(n, carry):
        at = [pl.multiple_of(plan[5 * n + i], SIZE) for i in range(1, 4)]
        one, other = transport(at[0]), faces(*at)
        for _ in other:
            next(one, None)
        lax.switch(plan[5 * n], kinds, plan[5 * n + 4])
        return carry

    lax.fori_loop(0, len(steps(slices)), step, 0)

    for f in range(FIELDS):

        def own(ref, slot):
            at = slot * SIZE + f * 256 + column
            return jnp.concatenate([ref[pl.ds(at + 1280 * p, 32, 8), :] for p in (0, 1)], axis=0)

        begin, end = own(ss, mine), own(ss, mine + 1)
        middle = own(uu, mine) + 0.5 * (begin + end)
        x = jnp.concatenate([begin, middle, end], axis=1)
        r = jnp.dot(back[...], split_rows(x), preferred_element_type=f32)
        for i in range(3):
            out[i, 64 * f : 64 * f + 64, :] = r[:, 128 * i : 128 * i + 128]


def join_kernel(values, viscosity, out):
    out[0:ROWS, :] = values[...]
    out[ROWS : ROWS + 8, :] = jnp.broadcast_to(viscosity[...], (8, 128))


def local_whole_grid(slices):
    def local(initial, viscosity, flux_jacobian):
        vmem = pl.BlockSpec(memory_space=pltpu.VMEM)
        block = pl.pallas_call(
            join_kernel,
            out_shape=jax.ShapeDtypeStruct((ROWS + 8, 128), jnp.float32),
            in_specs=[vmem, vmem],
            out_specs=vmem,
        )(initial.reshape(ROWS, 128), viscosity.reshape(1, 128))
        near = [block]
        for k in range(1, 4):
            near.append(lax.ppermute(block, "sy", [(i, i ^ k) for i in range(4)]))
        gathered = near + [lax.ppermute(b, "sx", [(0, 1), (1, 0)]) for b in near]

        plan = [(ORDER.index(kind), at * SIZE, at * SIZE, at * SIZE, t) for kind, at, t in steps(slices)]
        plan = jnp.asarray(np.array(plan, np.int32).reshape(-1))

        into, back, blocks = modal_tables()
        tables = jnp.asarray(blocks, jnp.float32)
        matrix = sum(
            flux_jacobian[d][None, :, None, :, None] * tables[:, d, None, :, None, :] for d in range(3)
        ).reshape(2, 160, 160)

        smem = pl.BlockSpec(memory_space=pltpu.SMEM)
        anywhere = pl.BlockSpec(memory_space=pl.ANY)

        def scratch(rows):
            return pltpu.VMEM((rows, 128), jnp.float32)

        out = pl.pallas_call(
            lambda plan, *refs: whole_grid_kernel(slices, plan, *refs),
            out_shape=jax.ShapeDtypeStruct((3, ROWS, 128), jnp.float32),
            in_specs=[smem] + [anywhere] * 8 + [vmem] * 3,
            out_specs=vmem,
            scratch_shapes=[
                scratch((slices + 1) * SIZE),
                scratch((slices + 1) * SIZE),
                scratch(slices * SIZE),
                scratch(slices * SIZE),
                scratch((slices + 3) * SIZE),
                scratch(slices * SIZE),
                *[scratch(SIZE)] * 7,
                scratch(SIZE),
                scratch(3840),
                pltpu.VMEM((2, 160, 480), jnp.bfloat16),
                *[scratch(8 * len(LEVELS))] * 4,
                scratch(8),
                pltpu.VMEM((8, ROWS + 8, 128), jnp.float32),
                pltpu.SemaphoreType.DMA((8,)),
            ],
            compiler_params=pltpu.CompilerParams(vmem_limit_bytes=58 << 20),
        )(plan, *gathered, matrix, three_pass(into), three_pass(back))
        return out.reshape(1, 3, 1, 1, FIELDS, 64, 128)

    return local


def solution(mesh):
    grid = (mesh.shape["sx"], mesh.shape["sy"])
    slices = mesh.shape["tm"]
    local = local_whole_grid(slices) if grid == (2, 4) and slices <= 4 else local_exchanging
    return jax.shard_map(
        local,
        mesh=mesh,
        in_specs=(P("sx", "sy", None, None, None), P("sx", "sy", None), P()),
        out_specs=P("tm", None, "sx", "sy", None, None, None),
        check_vma=False,
    )
```

```python
import math

import jax
import jax.numpy as jnp
import numpy as np
from jax import lax
from jax.experimental import pallas as pl
from jax.experimental.pallas import tpu as pltpu
from jax.sharding import PartitionSpec as P

ITERS = 2
JF = 3
JC = 2


SIGMA = 3.0
BETA = 0.5
STEP = 0.1
HALF_STEP = 0.05
TWO_THIRDS = 2.0 / 3.0
ONE_THIRD = 1.0 / 3.0
HIGHEST = lax.Precision.HIGHEST
WEIGHTS = ((5.0 / 24.0, 1.0 / 3.0, -1.0 / 24.0), (-1.0 / 24.0, 1.0 / 3.0, 5.0 / 24.0))


def passed_along(block, axis, distance):
    devices = range(lax.axis_size(axis))
    route = [(i - distance, i) for i in devices if i - distance in devices]
    return lax.ppermute(block, axis, route)


def kron_three(first, second, third):
    return jnp.kron(jnp.kron(first, second), third)


def node_tables():
    places = jnp.arange(4)
    row = places[:, None]
    column = places[None, :]
    identity = (row == column).astype(jnp.float32)
    upper = (row + 1 == column).astype(jnp.float32)
    border = identity * ((row == 0) | (row == 3)).astype(jnp.float32)
    line_laplace = 2.0 * identity - upper - upper.T - border
    line_grad = 0.5 * upper - 0.5 * upper.T
    laplace = (
        kron_three(line_laplace, identity, identity)
        + kron_three(identity, line_laplace, identity)
        + kron_three(identity, identity, line_laplace)
        + SIGMA * jnp.eye(64, dtype=jnp.float32)
    )
    grads = jnp.stack(
        [
            kron_three(line_grad, identity, identity),
            kron_three(identity, line_grad, identity),
            kron_three(identity, identity, line_grad),
        ]
    )
    weighting = jnp.where(row == 0, 0.5, math.sqrt(0.5)).astype(jnp.float32)
    cosine = weighting * jnp.cos(
        math.pi * row.astype(jnp.float32) * (2.0 * column.astype(jnp.float32) + 1.0) / 8.0
    )
    basis = kron_three(cosine, cosine, cosine)
    line_eigen = 2.0 - 2.0 * jnp.cos(math.pi * places.astype(jnp.float32) / 4.0)
    spectrum = (
        line_eigen[:, None, None] + line_eigen[None, :, None] + line_eigen[None, None, :]
    ).reshape(64) + SIGMA
    return (laplace, grads, basis, spectrum)


def previous(array, axis):
    widths = [(0, 0)] * array.ndim
    widths[axis] = (1, 0)
    return lax.slice_in_dim(jnp.pad(array, widths), 0, array.shape[axis], axis=axis)


def following(array, axis):
    widths = [(0, 0)] * array.ndim
    widths[axis] = (0, 1)
    return lax.slice_in_dim(jnp.pad(array, widths), 1, array.shape[axis] + 1, axis=axis)


def place(before, after, axis):
    empty = jnp.zeros_like(before)
    return jnp.stack([before, empty, empty, after], axis=axis)


def neighbours(field):
    lattice = field.reshape(field.shape[:4] + (4, 4, 4) + field.shape[-1:])
    high_x = lattice[:, :, :, :, 3]
    low_x = lattice[:, :, :, :, 0]
    from_west = passed_along(high_x[:, -1], "sx", 1)
    from_east = passed_along(low_x[:, 0], "sx", -1)
    before_x = jnp.concatenate([from_west[:, None], high_x[:, :-1]], axis=1)
    after_x = jnp.concatenate([low_x[:, 1:], from_east[:, None]], axis=1)
    high_y = lattice[:, :, :, :, :, 3]
    low_y = lattice[:, :, :, :, :, 0]
    from_south = passed_along(high_y[:, :, -1], "sy", 1)
    from_north = passed_along(low_y[:, :, 0], "sy", -1)
    before_y = jnp.concatenate([from_south[:, :, None], high_y[:, :, :-1]], axis=2)
    after_y = jnp.concatenate([low_y[:, :, 1:], from_north[:, :, None]], axis=2)
    along_x = place(before_x, after_x, 4)
    along_y = place(before_y, after_y, 5)
    along_z = place(previous(lattice[..., 3, :], 6), following(lattice[..., 0, :], 6), 6)
    return (along_x + along_y + along_z).reshape(field.shape)


def apply_operator(field, coeff, flux_jacobian, laplace, grads, coupled):
    volume = jnp.einsum("mn,bxyfnz->bxyfmz", laplace, field, precision=HIGHEST)
    slopes = jnp.einsum("dmn,bxyfnz->dbxyfmz", grads, field, precision=HIGHEST)
    transport = jnp.einsum("dgf,dbxyfmz->bxygmz", flux_jacobian, slopes, precision=HIGHEST)
    return coeff * (volume - BETA * coupled) + transport


def precondition(residue, coeff, basis, spectrum, step):
    inverse = 1.0 / (1.0 + step * coeff * spectrum[:, None])
    modes = jnp.einsum("kn,bxyfnz->bxyfkz", basis, residue, precision=HIGHEST)
    return jnp.einsum("kn,bxyfkz->bxyfnz", basis, modes * inverse, precision=HIGHEST)


def block_jacobi(target, begin, force, step, turns, operate, solve):
    field = begin
    image = -force
    for turn in range(turns):
        if turn > 0:
            image = operate(field)
        field = field + solve(target - field - step * image, step)
    return field


def local_exchanging(initial, viscosity, flux_jacobian):
    laplace, grads, basis, spectrum = node_tables()
    coeff = viscosity[None, :, :, None, None, :]
    first_slice = lax.axis_index("tm") == 0

    def operate(field):
        return apply_operator(field, coeff, flux_jacobian, laplace, grads, neighbours(field))

    def solve(residue, step):
        return precondition(residue, coeff, basis, spectrum, step)

    start = initial[None]
    force_zero = -operate(start)
    values = [start, start, start]
    forces = [force_zero, force_zero, force_zero]
    for sweep in range(ITERS):
        old = list(forces)
        for node in range(2):
            weight = WEIGHTS[node]
            integral = STEP * (weight[0] * old[0] + weight[1] * old[1] + weight[2] * old[2])
            target = values[node] - HALF_STEP * old[node + 1] + integral
            values[node + 1] = block_jacobi(
                target, values[node + 1], old[node + 1], HALF_STEP, JF, operate, solve
            )
            forces[node + 1] = -operate(values[node + 1])
        correction = STEP * (TWO_THIRDS * forces[1] - ONE_THIRD * forces[0] - ONE_THIRD * forces[2])
        offset = -STEP * forces[2] + HALF_STEP * (forces[0] + forces[2]) + correction
        end_value = values[2]
        end_force = forces[2]

        def chain_turn(turn, carry):
            coarse_start, coarse_end = carry
            coarse_end = block_jacobi(
                coarse_start + offset, end_value, end_force, STEP, JC, operate, solve
            )
            passed = passed_along(coarse_end, "tm", 1)
            return (jnp.where(first_slice, start, passed), coarse_end)

        coarse_start, coarse_end = lax.fori_loop(0, lax.axis_size("tm"), chain_turn, (start, start))
        if sweep + 1 < ITERS:
            both = -operate(jnp.concatenate([coarse_start, coarse_end], axis=0))
            force_start = both[:1]
            force_end = both[1:]
            delta_start = force_start - forces[0]
            delta_end = force_end - forces[2]
            forces = [
                forces[0] + delta_start,
                forces[1] + 0.5 * (delta_start + delta_end),
                forces[2] + delta_end,
            ]
        move_start = coarse_start - values[0]
        move_end = coarse_end - values[2]
        values = [
            values[0] + move_start,
            values[1] + 0.5 * (move_start + move_end),
            values[2] + move_end,
        ]
    return jnp.stack(values, axis=1)


FIELDS = 5
ROWS = 320
SIZE = 2560
FACE = np.array([0.5] + [math.sqrt(0.5) * math.cos(math.pi * k / 8.0) for k in (1, 2, 3)])
PICK_1 = 4.0 * FACE[1] ** 2
PICK_3 = 4.0 * FACE[3] ** 2
MODES = [
    (a, b, c)
    for parity in (0, 1)
    for a in range(4)
    for b in range(4)
    for c in range(4)
    if (a + b + c) % 2 == parity
]
PLACE = {mode: (i // 32) * 160 + i % 32 for i, mode in enumerate(MODES)}
LEVELS = sorted({tuple(sorted(mode)) for mode in MODES})


def level(a, b, c):
    return LEVELS.index(tuple(sorted((a, b, c))))


def eigen(levels):
    line = [2.0 - 2.0 * math.cos(math.pi * k / 4.0) for k in range(4)]
    return sum(line[k] for k in levels) + SIGMA


def modal_tables():
    j = np.arange(4)
    cosine = np.cos(math.pi * j[:, None] * (2.0 * j[None, :] + 1.0) / 8.0)
    cosine *= np.where(j == 0, 0.5, math.sqrt(0.5))[:, None]
    basis = np.kron(np.kron(cosine, cosine), cosine)
    scale = np.kron(np.kron(FACE, FACE), FACE)
    order = [16 * a + 4 * b + c for a, b, c in MODES]
    into = (basis / scale[:, None])[order]
    back = (basis * scale[:, None])[order].T
    upper = np.eye(4, k=1)
    slope = 0.5 * upper - 0.5 * upper.T
    one = np.eye(4)
    grads = [
        np.kron(np.kron(slope, one), one),
        np.kron(np.kron(one, slope), one),
        np.kron(np.kron(one, one), slope),
    ]
    modal = np.stack([into @ grad @ back for grad in grads])
    blocks = np.stack([modal[:, 32:, :32], modal[:, :32, 32:]])
    return into, back, HALF_STEP * blocks


def three_pass(matrix):
    high = matrix.astype(jnp.bfloat16)
    low = (matrix - high.astype(np.float64)).astype(jnp.bfloat16)
    return jnp.asarray(np.concatenate([high, low, high], axis=1))


def split_rows(x):
    high = x.astype(jnp.bfloat16)
    low = (x - high.astype(jnp.float32)).astype(jnp.bfloat16)
    return jnp.concatenate([high, high, low], axis=0)


ORDER = [9, 8, 7, 10, 11, 12, 13, 0, 1, 2, 3, 4, 5, 6]


def steps(slices):
    work, mid, copy = slices, slices + 1, slices + 2
    plan = [(0, work, 0), (1, work, 0), (2, work, 0), (3, work, 0), (4, work, 0), (5, work, 0)]
    plan += [(6, mid, 0)]
    for t in range(slices):
        plan += [(7, work, t), (8, copy, t)]
    for kind in (9, 10, 9, 11):
        plan += [(kind, t, t) for t in range(slices)]
    plan += [(12, t, t) for t in reversed(range(slices))]
    plan += [(13, work, t) for t in range(slices)]
    return plan


def whole_grid_kernel(slices, plan, *refs):
    gathered, refs = refs[:8], refs[8:]
    matrix, into, back, out, *refs = refs
    ss, gg, tt, pp, vv, uu, first, quad, base, zed, c0, hga, c2, tr, g, m, dh, dd, de, el, cc, gin, sems = refs
    f32 = jnp.float32
    work, mid, copy = slices * SIZE, (slices + 1) * SIZE, (slices + 2) * SIZE

    copies = [pltpu.make_async_copy(gathered[k], gin.at[k], sems.at[k]) for k in range(8)]
    for copy_in in copies:
        copy_in.start()
    x_here, y_here = lax.axis_index("sx"), lax.axis_index("sy")
    mine, column = lax.axis_index("tm"), 4 * x_here + y_here
    places = [(x_here ^ (k // 4)) * 4 + (y_here ^ (k % 4)) for k in range(8)]
    for p in range(2):
        whole = matrix[p]
        high = whole.astype(jnp.bfloat16).astype(f32)
        m[p] = jnp.concatenate([high, whole - high, high], axis=1).astype(jnp.bfloat16)
    for copy_in in copies:
        copy_in.wait()
    for k in range(8):
        cc[pl.ds(places[k], 1), :] = gin[k, 320:321, :]
    visc = cc[...]
    for i, levels in enumerate(LEVELS):
        lam = (HALF_STEP * eigen(levels)) * visc
        el[8 * i : 8 * i + 8, :] = lam
        dh[8 * i : 8 * i + 8, :] = 1.0 / (1.0 + lam)
        dd[8 * i : 8 * i + 8, :] = 1.0 / (1.0 + 2.0 * lam)
        de[8 * i : 8 * i + 8, :] = 2.0 / (1.0 + 2.0 * lam)
    for k in range(0, 8, 2):
        for f in range(FIELDS):
            x = jnp.concatenate([gin[k + i, 64 * f : 64 * f + 64, :] for i in (0, 1)], axis=1)
            r = jnp.dot(into[...], split_rows(x), preferred_element_type=f32)
            for i in (0, 1):
                for p in (0, 1):
                    at = p * 1280 + f * 256 + places[k + i]
                    part = r[32 * p : 32 * p + 32, 128 * i : 128 * i + 128]
                    ss[pl.ds(at, 32, 8), :] = part
                    vv[pl.ds(work + at, 32, 8), :] = part

    sub = lax.broadcasted_iota(jnp.int32, (8, 128), 0)
    lane = lax.broadcasted_iota(jnp.int32, (8, 128), 1)
    tau = jnp.where(sub >= 4, 1.0, -1.0).astype(f32)
    tau_1, tau_3 = PICK_1 * tau, PICK_3 * tau
    y_first, y_last = sub % 4 == 0, sub % 4 == 3
    z_first, z_last = lane == 0, lane == 127
    scaled = (HALF_STEP * BETA * 0.25) * visc

    def transport(at):
        for half in range(2):
            for p in range(2):
                begin = at + (p * 1280 + 4 * half)
                x = jnp.concatenate([vv[pl.ds(begin + i, 160, 8), :] for i in range(4)], axis=1)
                r = jnp.dot(m[p], split_rows(x), preferred_element_type=f32)
                for i in range(4):
                    row = (1 - p) * 1280 + 4 * half + i
                    tr[pl.ds(row, 160, 8), :] = r[:, 128 * i : 128 * i + 128]
                yield

    def faces(at_x, at_y, at_z):
        def ld(at, a, b, c):
            return vv[pl.ds(at + (256 * f + 8 * PLACE[a, b, c]), 8), :]

        for f in range(FIELDS):
            for p in range(4):
                for q in range(4):
                    i = 8 * (16 * f + 4 * p + q)
                    even = ld(at_x, 0, p, q) + ld(at_x, 2, p, q)
                    odd = tau_1 * ld(at_x, 1, p, q) + tau_3 * ld(at_x, 3, p, q)
                    met = pltpu.roll(even + odd, 4, 0)
                    g[i : i + 8, :] = met
                    g[640 + i : 648 + i, :] = tau * met
                    even = ld(at_y, p, 0, q) + ld(at_y, p, 2, q)
                    odd = PICK_1 * ld(at_y, p, 1, q) + PICK_3 * ld(at_y, p, 3, q)
                    low = jnp.where(y_first, 0.0, pltpu.roll(even - odd, 1, 0))
                    high = jnp.where(y_last, 0.0, pltpu.roll(even + odd, 7, 0))
                    g[1280 + i : 1288 + i, :] = low + high
                    g[1920 + i : 1928 + i, :] = low - high
                    even = ld(at_z, p, q, 0) + ld(at_z, p, q, 2)
                    odd = PICK_1 * ld(at_z, p, q, 1) + PICK_3 * ld(at_z, p, q, 3)
                    low = jnp.where(z_first, 0.0, pltpu.roll(even - odd, 1, 1))
                    high = jnp.where(z_last, 0.0, pltpu.roll(even + odd, 127, 1))
                    g[2560 + i : 2568 + i, :] = low + high
                    g[3200 + i : 3208 + i, :] = low - high
            yield

    def finish(store):
        def field(f, carry):
            at = pl.multiple_of(f * 256, 256)
            gat = pl.multiple_of(f * 128, 128)
            for pa in range(2):
                for pb in range(2):
                    gx = {
                        (b, c): g[pl.ds(gat + (640 * pa + 8 * (4 * b + c)), 8), :]
                        for b in (pb, pb + 2)
                        for c in range(4)
                    }
                    gy = {
                        (a, c): g[pl.ds(gat + (1280 + 640 * pb + 8 * (4 * a + c)), 8), :]
                        for a in (pa, pa + 2)
                        for c in range(4)
                    }
                    for a in (pa, pa + 2):
                        for b in (pb, pb + 2):
                            gz = [
                                g[pl.ds(gat + (2560 + 640 * pc + 8 * (4 * a + b)), 8), :]
                                for pc in range(2)
                            ]
                            for c in range(4):
                                row = 8 * PLACE[a, b, c]
                                n = gx[b, c] + gy[a, c] + gz[c % 2]
                                image = tr[pl.ds(at + row, 8), :] - scaled * n
                                store((at, row), level(a, b, c), image)
            return carry

        lax.fori_loop(0, FIELDS, field, 0)

    def ld(ref, row, start=0, more=0):
        return ref[pl.ds(pl.multiple_of(start + row[0], 256) + (more + row[1]), 8), :]

    def put(ref, row, x, start=0, more=0):
        ref[pl.ds(pl.multiple_of(start + row[0], 256) + (more + row[1]), 8), :] = x

    def tab(ref, i):
        return ref[8 * i : 8 * i + 8, :]

    def kind_0(t):
        def store(row, i, image):
            put(gg, row, image)
            start = ld(ss, row)
            put(tt, row, start)
            put(vv, row, tab(dh, i) * (start - image), 0, work)

        finish(store)

    def kind_1(t):
        def store(row, i, image):
            put(vv, row, tab(dh, i) * (ld(ss, row) - image), 0, work)

        finish(store)

    def kind_2(t):
        def store(row, i, image):
            u = tab(dh, i) * (ld(ss, row) - image)
            put(first, row, u)
            put(vv, row, tab(dh, i) * (u - ld(gg, row)), 0, work)

        finish(store)

    def kind_3(t):
        def store(row, i, image):
            put(vv, row, tab(dh, i) * (ld(first, row) - image), 0, work)

        finish(store)

    def kind_4(t):
        def store(row, i, image):
            u1 = ld(first, row)
            u2 = tab(dh, i) * (u1 - image)
            start = ld(ss, row)
            put(vv, row, u1 - 0.5 * (start + u2), 0, mid)
            mix = (4.0 / 3.0) * u1 + (1.0 / 3.0) * u2
            put(vv, row, mix, 0, work)
            q = u2 + u2 - mix
            put(quad, row, q)
            put(base, row, tab(el, i) * (q - (1.0 / 3.0) * start) - (1.0 / 3.0) * ld(gg, row))

        finish(store)

    def kind_5(t):
        def store(row, i, image):
            z = ld(base, row) - image
            put(zed, row, z)
            put(vv, row, tab(de, i) * (ld(ss, row) + z) - ld(quad, row), 0, work)

        finish(store)

    def kind_6(t):
        def store(row, i, image):
            put(hga, row, image)
            c = (1.0 / 3.0) * (tab(el, i) * ld(vv, row, 0, mid) + image)
            put(c0, row, c)
            put(c2, row, c + c)

        finish(store)

    def kind_7(t):
        at = t * SIZE

        def store(row, i, image):
            s = tab(dd, i) * (ld(ss, row, at) + ld(base, row) - image)
            put(ss, row, s, at, SIZE)
            put(vv, row, s, 0, copy)
            put(vv, row, tab(de, i) * (s + ld(zed, row)) - ld(quad, row), 0, work)

        finish(store)

    def kind_8(t):
        at = t * SIZE

        def store(row, i, image):
            put(gg, row, image, at, SIZE)
            s = ld(ss, row, at)
            old = ld(gg, row, at)
            phi = 0.25 * (tab(el, i) * (ld(ss, row, at, SIZE) - s) + image - old)
            target = s + phi + ld(c0, row)
            put(tt, row, target, at, SIZE)
            put(pp, row, phi - ld(c2, row), at)
            put(vv, row, tab(dh, i) * (target - ld(hga, row) - 0.5 * (old + image)), at)

        finish(store)

    def kind_9(t):
        at = t * SIZE

        def store(row, i, image):
            put(vv, row, tab(dh, i) * (ld(tt, row, at, SIZE) - image), at)

        finish(store)

    def kind_10(t):
        at = t * SIZE

        def store(row, i, image):
            u = tab(dh, i) * (ld(tt, row, at, SIZE) - image)
            put(uu, row, u, at)
            target = u + ld(pp, row, at)
            put(tt, row, target, at, SIZE)
            put(vv, row, tab(dh, i) * (target - ld(gg, row, at, SIZE)), at)

        finish(store)

    def kind_11(t):
        at = t * SIZE

        def store(row, i, image):
            u1 = ld(uu, row, at)
            u2 = tab(dh, i) * (ld(tt, row, at, SIZE) - image)
            s = ld(ss, row, at)
            mix = (4.0 / 3.0) * u1 + (1.0 / 3.0) * u2
            put(vv, row, mix, at)
            q = u2 + u2 - mix
            put(pp, row, q, at)
            old = ld(gg, row, at)
            put(tt, row, tab(el, i) * (q - (1.0 / 3.0) * s) - (1.0 / 3.0) * old, at, SIZE)

        finish(store)

    def kind_12(t):
        at = t * SIZE

        def store(row, i, image):
            z = ld(tt, row, at, SIZE) - image
            put(gg, row, z, at)
            put(vv, row, tab(de, i) * (ld(ss, row) + z) - ld(pp, row, at), 0, work)

        finish(store)

    def kind_13(t):
        at = t * SIZE
        later = jnp.minimum(t + 1, slices - 1) * SIZE

        def store(row, i, image):
            s = tab(dd, i) * (ld(tt, row, at) + ld(tt, row, at, SIZE) - image)
            put(tt, row, s, at, SIZE)
            z = ld(gg, row, later)
            put(vv, row, tab(de, i) * (s + z) - ld(pp, row, later), 0, work)

        finish(store)

    kinds = [kind_9, kind_8, kind_7, kind_10, kind_11, kind_12, kind_13]
    kinds += [kind_0, kind_1, kind_2, kind_3, kind_4, kind_5, kind_6]

    def step(n, carry):
        at = [pl.multiple_of(plan[5 * n + i], SIZE) for i in range(1, 4)]
        one, other = transport(at[0]), faces(*at)
        for _ in other:
            next(one, None)
        lax.switch(plan[5 * n], kinds, plan[5 * n + 4])
        return carry

    lax.fori_loop(0, len(steps(slices)), step, 0)

    for f in range(FIELDS):

        def own(ref, slot):
            at = slot * SIZE + f * 256 + column
            return jnp.concatenate([ref[pl.ds(at + 1280 * p, 32, 8), :] for p in (0, 1)], axis=0)

        begin, end = own(tt, mine), own(tt, mine + 1)
        fine_end = 0.5 * (own(pp, mine) + own(vv, mine))
        middle = own(uu, mine) + 0.5 * (begin - own(ss, mine) + end - fine_end)
        x = jnp.concatenate([begin, middle, end], axis=1)
        r = jnp.dot(back[...], split_rows(x), preferred_element_type=f32)
        for i in range(3):
            out[i, 64 * f : 64 * f + 64, :] = r[:, 128 * i : 128 * i + 128]


def join_kernel(values, viscosity, out):
    out[0:ROWS, :] = values[...]
    out[ROWS : ROWS + 8, :] = jnp.broadcast_to(viscosity[...], (8, 128))


def local_whole_grid(slices):
    def local(initial, viscosity, flux_jacobian):
        vmem = pl.BlockSpec(memory_space=pltpu.VMEM)
        block = pl.pallas_call(
            join_kernel,
            out_shape=jax.ShapeDtypeStruct((ROWS + 8, 128), jnp.float32),
            in_specs=[vmem, vmem],
            out_specs=vmem,
        )(initial.reshape(ROWS, 128), viscosity.reshape(1, 128))
        near = [block]
        for k in range(1, 4):
            near.append(lax.ppermute(block, "sy", [(i, i ^ k) for i in range(4)]))
        gathered = near + [lax.ppermute(b, "sx", [(0, 1), (1, 0)]) for b in near]

        plan = [(ORDER.index(kind), at * SIZE, at * SIZE, at * SIZE, t) for kind, at, t in steps(slices)]
        plan = jnp.asarray(np.array(plan, np.int32).reshape(-1))

        into, back, blocks = modal_tables()
        tables = jnp.asarray(blocks, jnp.float32)
        matrix = sum(
            flux_jacobian[d][None, :, None, :, None] * tables[:, d, None, :, None, :] for d in range(3)
        ).reshape(2, 160, 160)

        smem = pl.BlockSpec(memory_space=pltpu.SMEM)
        hbm = pl.BlockSpec(memory_space=pltpu.HBM)

        def scratch(rows):
            return pltpu.VMEM((rows, 128), jnp.float32)

        out = pl.pallas_call(
            lambda plan, *refs: whole_grid_kernel(slices, plan, *refs),
            out_shape=jax.ShapeDtypeStruct((3, ROWS, 128), jnp.float32),
            in_specs=[smem] + [hbm] * 8 + [vmem] * 3,
            out_specs=vmem,
            scratch_shapes=[
                scratch((slices + 1) * SIZE),
                scratch((slices + 1) * SIZE),
                scratch((slices + 1) * SIZE),
                scratch(slices * SIZE),
                scratch((slices + 3) * SIZE),
                scratch(slices * SIZE),
                *[scratch(SIZE)] * 7,
                scratch(SIZE),
                scratch(3840),
                pltpu.VMEM((2, 160, 480), jnp.bfloat16),
                *[scratch(8 * len(LEVELS))] * 4,
                scratch(8),
                pltpu.VMEM((8, ROWS + 8, 128), jnp.float32),
                pltpu.SemaphoreType.DMA((8,)),
            ],
            compiler_params=pltpu.CompilerParams(vmem_limit_bytes=58 << 20),
        )(plan, *gathered, matrix, three_pass(into), three_pass(back))
        return out.reshape(1, 3, 1, 1, FIELDS, 64, 128)

    return local


def solution(mesh):
    grid = (mesh.shape["sx"], mesh.shape["sy"])
    slices = mesh.shape["tm"]
    local = local_whole_grid(slices) if grid == (2, 4) and slices <= 4 else local_exchanging
    return jax.shard_map(
        local,
        mesh=mesh,
        in_specs=(P("sx", "sy", None, None, None), P("sx", "sy", None), P()),
        out_specs=P("tm", None, "sx", "sy", None, None, None),
        check_vma=False,
    )
```

```python
import math

import jax
import jax.numpy as jnp
import numpy as np
from jax import lax
from jax.experimental import pallas as pl
from jax.experimental.pallas import tpu as pltpu
from jax.sharding import PartitionSpec as P

ITERS = 2
JF = 3
JC = 2


SIGMA = 3.0
BETA = 0.5
STEP = 0.1
HALF_STEP = 0.05
TWO_THIRDS = 2.0 / 3.0
ONE_THIRD = 1.0 / 3.0
HIGHEST = lax.Precision.HIGHEST
WEIGHTS = ((5.0 / 24.0, 1.0 / 3.0, -1.0 / 24.0), (-1.0 / 24.0, 1.0 / 3.0, 5.0 / 24.0))


def passed_along(block, axis, distance):
    devices = range(lax.axis_size(axis))
    route = [(i - distance, i) for i in devices if i - distance in devices]
    return lax.ppermute(block, axis, route)


def kron_three(first, second, third):
    return jnp.kron(jnp.kron(first, second), third)


def node_tables():
    places = jnp.arange(4)
    row = places[:, None]
    column = places[None, :]
    identity = (row == column).astype(jnp.float32)
    upper = (row + 1 == column).astype(jnp.float32)
    border = identity * ((row == 0) | (row == 3)).astype(jnp.float32)
    line_laplace = 2.0 * identity - upper - upper.T - border
    line_grad = 0.5 * upper - 0.5 * upper.T
    laplace = (
        kron_three(line_laplace, identity, identity)
        + kron_three(identity, line_laplace, identity)
        + kron_three(identity, identity, line_laplace)
        + SIGMA * jnp.eye(64, dtype=jnp.float32)
    )
    grads = jnp.stack(
        [
            kron_three(line_grad, identity, identity),
            kron_three(identity, line_grad, identity),
            kron_three(identity, identity, line_grad),
        ]
    )
    weighting = jnp.where(row == 0, 0.5, math.sqrt(0.5)).astype(jnp.float32)
    cosine = weighting * jnp.cos(
        math.pi * row.astype(jnp.float32) * (2.0 * column.astype(jnp.float32) + 1.0) / 8.0
    )
    basis = kron_three(cosine, cosine, cosine)
    line_eigen = 2.0 - 2.0 * jnp.cos(math.pi * places.astype(jnp.float32) / 4.0)
    spectrum = (
        line_eigen[:, None, None] + line_eigen[None, :, None] + line_eigen[None, None, :]
    ).reshape(64) + SIGMA
    return (laplace, grads, basis, spectrum)


def previous(array, axis):
    widths = [(0, 0)] * array.ndim
    widths[axis] = (1, 0)
    return lax.slice_in_dim(jnp.pad(array, widths), 0, array.shape[axis], axis=axis)


def following(array, axis):
    widths = [(0, 0)] * array.ndim
    widths[axis] = (0, 1)
    return lax.slice_in_dim(jnp.pad(array, widths), 1, array.shape[axis] + 1, axis=axis)


def place(before, after, axis):
    empty = jnp.zeros_like(before)
    return jnp.stack([before, empty, empty, after], axis=axis)


def neighbours(field):
    lattice = field.reshape(field.shape[:4] + (4, 4, 4) + field.shape[-1:])
    high_x = lattice[:, :, :, :, 3]
    low_x = lattice[:, :, :, :, 0]
    from_west = passed_along(high_x[:, -1], "sx", 1)
    from_east = passed_along(low_x[:, 0], "sx", -1)
    before_x = jnp.concatenate([from_west[:, None], high_x[:, :-1]], axis=1)
    after_x = jnp.concatenate([low_x[:, 1:], from_east[:, None]], axis=1)
    high_y = lattice[:, :, :, :, :, 3]
    low_y = lattice[:, :, :, :, :, 0]
    from_south = passed_along(high_y[:, :, -1], "sy", 1)
    from_north = passed_along(low_y[:, :, 0], "sy", -1)
    before_y = jnp.concatenate([from_south[:, :, None], high_y[:, :, :-1]], axis=2)
    after_y = jnp.concatenate([low_y[:, :, 1:], from_north[:, :, None]], axis=2)
    along_x = place(before_x, after_x, 4)
    along_y = place(before_y, after_y, 5)
    along_z = place(previous(lattice[..., 3, :], 6), following(lattice[..., 0, :], 6), 6)
    return (along_x + along_y + along_z).reshape(field.shape)


def apply_operator(field, coeff, flux_jacobian, laplace, grads, coupled):
    volume = jnp.einsum("mn,bxyfnz->bxyfmz", laplace, field, precision=HIGHEST)
    slopes = jnp.einsum("dmn,bxyfnz->dbxyfmz", grads, field, precision=HIGHEST)
    transport = jnp.einsum("dgf,dbxyfmz->bxygmz", flux_jacobian, slopes, precision=HIGHEST)
    return coeff * (volume - BETA * coupled) + transport


def precondition(residue, coeff, basis, spectrum, step):
    inverse = 1.0 / (1.0 + step * coeff * spectrum[:, None])
    modes = jnp.einsum("kn,bxyfnz->bxyfkz", basis, residue, precision=HIGHEST)
    return jnp.einsum("kn,bxyfkz->bxyfnz", basis, modes * inverse, precision=HIGHEST)


def block_jacobi(target, begin, force, step, turns, operate, solve):
    field = begin
    image = -force
    for turn in range(turns):
        if turn > 0:
            image = operate(field)
        field = field + solve(target - field - step * image, step)
    return field


def local_exchanging(initial, viscosity, flux_jacobian):
    laplace, grads, basis, spectrum = node_tables()
    coeff = viscosity[None, :, :, None, None, :]
    first_slice = lax.axis_index("tm") == 0

    def operate(field):
        return apply_operator(field, coeff, flux_jacobian, laplace, grads, neighbours(field))

    def solve(residue, step):
        return precondition(residue, coeff, basis, spectrum, step)

    start = initial[None]
    force_zero = -operate(start)
    values = [start, start, start]
    forces = [force_zero, force_zero, force_zero]
    for sweep in range(ITERS):
        old = list(forces)
        for node in range(2):
            weight = WEIGHTS[node]
            integral = STEP * (weight[0] * old[0] + weight[1] * old[1] + weight[2] * old[2])
            target = values[node] - HALF_STEP * old[node + 1] + integral
            values[node + 1] = block_jacobi(
                target, values[node + 1], old[node + 1], HALF_STEP, JF, operate, solve
            )
            forces[node + 1] = -operate(values[node + 1])
        correction = STEP * (TWO_THIRDS * forces[1] - ONE_THIRD * forces[0] - ONE_THIRD * forces[2])
        offset = -STEP * forces[2] + HALF_STEP * (forces[0] + forces[2]) + correction
        end_value = values[2]
        end_force = forces[2]

        def chain_turn(turn, carry):
            coarse_start, coarse_end = carry
            coarse_end = block_jacobi(
                coarse_start + offset, end_value, end_force, STEP, JC, operate, solve
            )
            passed = passed_along(coarse_end, "tm", 1)
            return (jnp.where(first_slice, start, passed), coarse_end)

        coarse_start, coarse_end = lax.fori_loop(0, lax.axis_size("tm"), chain_turn, (start, start))
        if sweep + 1 < ITERS:
            both = -operate(jnp.concatenate([coarse_start, coarse_end], axis=0))
            force_start = both[:1]
            force_end = both[1:]
            delta_start = force_start - forces[0]
            delta_end = force_end - forces[2]
            forces = [
                forces[0] + delta_start,
                forces[1] + 0.5 * (delta_start + delta_end),
                forces[2] + delta_end,
            ]
        move_start = coarse_start - values[0]
        move_end = coarse_end - values[2]
        values = [
            values[0] + move_start,
            values[1] + 0.5 * (move_start + move_end),
            values[2] + move_end,
        ]
    return jnp.stack(values, axis=1)


FIELDS = 5
ROWS = 320
SIZE = 2560
FACE = np.array([0.5] + [math.sqrt(0.5) * math.cos(math.pi * k / 8.0) for k in (1, 2, 3)])
PICK_1 = 4.0 * FACE[1] ** 2
PICK_3 = 4.0 * FACE[3] ** 2
MODES = [
    (a, b, c)
    for parity in (0, 1)
    for a in range(4)
    for b in range(4)
    for c in range(4)
    if (a + b + c) % 2 == parity
]
PLACE = {mode: (i // 32) * 160 + i % 32 for i, mode in enumerate(MODES)}
LEVELS = sorted({tuple(sorted(mode)) for mode in MODES})


def level(a, b, c):
    return LEVELS.index(tuple(sorted((a, b, c))))


def eigen(levels):
    line = [2.0 - 2.0 * math.cos(math.pi * k / 4.0) for k in range(4)]
    return sum(line[k] for k in levels) + SIGMA


def modal_tables():
    j = np.arange(4)
    cosine = np.cos(math.pi * j[:, None] * (2.0 * j[None, :] + 1.0) / 8.0)
    cosine *= np.where(j == 0, 0.5, math.sqrt(0.5))[:, None]
    basis = np.kron(np.kron(cosine, cosine), cosine)
    scale = np.kron(np.kron(FACE, FACE), FACE)
    order = [16 * a + 4 * b + c for a, b, c in MODES]
    into = (basis / scale[:, None])[order]
    back = (basis * scale[:, None])[order].T
    upper = np.eye(4, k=1)
    slope = 0.5 * upper - 0.5 * upper.T
    one = np.eye(4)
    grads = [
        np.kron(np.kron(slope, one), one),
        np.kron(np.kron(one, slope), one),
        np.kron(np.kron(one, one), slope),
    ]
    modal = np.stack([into @ grad @ back for grad in grads])
    blocks = np.stack([modal[:, 32:, :32], modal[:, :32, 32:]])
    return into, back, HALF_STEP * blocks


def three_pass(matrix):
    high = matrix.astype(jnp.bfloat16)
    low = (matrix - high.astype(np.float64)).astype(jnp.bfloat16)
    return jnp.asarray(np.concatenate([high, low, high], axis=1))


def split_rows(x):
    high = x.astype(jnp.bfloat16)
    low = (x - high.astype(jnp.float32)).astype(jnp.bfloat16)
    return jnp.concatenate([high, high, low], axis=0)


ORDER = [9, 8, 7, 10, 11, 12, 13, 0, 1, 2, 3, 4, 5, 6]


def steps(slices):
    work, mid, copy = slices, slices + 1, slices + 2
    plan = [(0, work, 0), (1, work, 0), (2, work, 0), (3, work, 0), (4, work, 0), (5, work, 0)]
    plan += [(6, mid, 0)]
    for t in range(slices):
        plan += [(7, work, t), (8, copy, t)]
    for kind in (9, 10, 9, 11):
        plan += [(kind, t, t) for t in range(slices)]
    plan += [(12, t, t) for t in reversed(range(slices))]
    plan += [(13, work, t) for t in range(slices)]
    return plan


def whole_grid_kernel(slices, plan, *refs):
    gathered, refs = refs[:8], refs[8:]
    matrix, into, back, out, *refs = refs
    ss, gg, tt, pp, vv, uu, first, quad, base, zed, c0, hga, c2, tr, g, m, dh, dd, de, el, cc, gin, sems = refs
    f32 = jnp.float32
    work, mid, copy = slices * SIZE, (slices + 1) * SIZE, (slices + 2) * SIZE

    copies = [pltpu.make_async_copy(gathered[k], gin.at[k], sems.at[k]) for k in range(8)]
    for copy_in in copies:
        copy_in.start()
    x_here, y_here = lax.axis_index("sx"), lax.axis_index("sy")
    mine, column = lax.axis_index("tm"), 4 * x_here + y_here
    places = [(x_here ^ (k // 4)) * 4 + (y_here ^ (k % 4)) for k in range(8)]
    for p in range(2):
        whole = matrix[p]
        high = whole.astype(jnp.bfloat16).astype(f32)
        m[p] = jnp.concatenate([high, whole - high, high], axis=1).astype(jnp.bfloat16)
    for copy_in in copies:
        copy_in.wait()
    for k in range(8):
        cc[pl.ds(places[k], 1), :] = gin[k, 320:321, :]
    visc = cc[...]
    for i, levels in enumerate(LEVELS):
        lam = (HALF_STEP * eigen(levels)) * visc
        el[8 * i : 8 * i + 8, :] = lam
        dh[8 * i : 8 * i + 8, :] = 1.0 / (1.0 + lam)
        dd[8 * i : 8 * i + 8, :] = 1.0 / (1.0 + 2.0 * lam)
        de[8 * i : 8 * i + 8, :] = 2.0 / (1.0 + 2.0 * lam)
    for k in range(0, 8, 2):
        for f in range(FIELDS):
            x = jnp.concatenate([gin[k + i, 64 * f : 64 * f + 64, :] for i in (0, 1)], axis=1)
            r = jnp.dot(into[...], split_rows(x), preferred_element_type=f32)
            for i in (0, 1):
                for p in (0, 1):
                    at = p * 1280 + f * 256 + places[k + i]
                    part = r[32 * p : 32 * p + 32, 128 * i : 128 * i + 128]
                    ss[pl.ds(at, 32, 8), :] = part
                    vv[pl.ds(work + at, 32, 8), :] = part

    sub = lax.broadcasted_iota(jnp.int32, (8, 128), 0)
    lane = lax.broadcasted_iota(jnp.int32, (8, 128), 1)
    tau = jnp.where(sub >= 4, 1.0, -1.0).astype(f32)
    tau_1, tau_3 = PICK_1 * tau, PICK_3 * tau
    y_first, y_last = sub % 4 == 0, sub % 4 == 3
    z_first, z_last = lane == 0, lane == 127
    scaled = (HALF_STEP * BETA * 0.25) * visc

    def transport(at):
        for half in range(2):
            for p in range(2):
                begin = at + (p * 1280 + 4 * half)
                x = jnp.concatenate([vv[pl.ds(begin + i, 160, 8), :] for i in range(4)], axis=1)
                r = jnp.dot(m[p], split_rows(x), preferred_element_type=f32)
                for i in range(4):
                    row = (1 - p) * 1280 + 4 * half + i
                    tr[pl.ds(row, 160, 8), :] = r[:, 128 * i : 128 * i + 128]
                yield

    def faces(at_x, at_y, at_z):
        def ld(at, a, b, c):
            return vv[pl.ds(at + (256 * f + 8 * PLACE[a, b, c]), 8), :]

        for f in range(FIELDS):
            for p in range(4):
                for q in range(4):
                    i = 8 * (16 * f + 4 * p + q)
                    even = ld(at_x, 0, p, q) + ld(at_x, 2, p, q)
                    odd = tau_1 * ld(at_x, 1, p, q) + tau_3 * ld(at_x, 3, p, q)
                    met = pltpu.roll(even + odd, 4, 0)
                    g[i : i + 8, :] = met
                    g[640 + i : 648 + i, :] = tau * met
                    even = ld(at_y, p, 0, q) + ld(at_y, p, 2, q)
                    odd = PICK_1 * ld(at_y, p, 1, q) + PICK_3 * ld(at_y, p, 3, q)
                    low = jnp.where(y_first, 0.0, pltpu.roll(even - odd, 1, 0))
                    high = jnp.where(y_last, 0.0, pltpu.roll(even + odd, 7, 0))
                    g[1280 + i : 1288 + i, :] = low + high
                    g[1920 + i : 1928 + i, :] = low - high
                    even = ld(at_z, p, q, 0) + ld(at_z, p, q, 2)
                    odd = PICK_1 * ld(at_z, p, q, 1) + PICK_3 * ld(at_z, p, q, 3)
                    low = jnp.where(z_first, 0.0, pltpu.roll(even - odd, 1, 1))
                    high = jnp.where(z_last, 0.0, pltpu.roll(even + odd, 127, 1))
                    g[2560 + i : 2568 + i, :] = low + high
                    g[3200 + i : 3208 + i, :] = low - high
            yield

    def finish(store):
        def field(f, carry):
            at = pl.multiple_of(f * 256, 256)
            gat = pl.multiple_of(f * 128, 128)
            for pa in range(2):
                for pb in range(2):
                    gx = {
                        (b, c): g[pl.ds(gat + (640 * pa + 8 * (4 * b + c)), 8), :]
                        for b in (pb, pb + 2)
                        for c in range(4)
                    }
                    gy = {
                        (a, c): g[pl.ds(gat + (1280 + 640 * pb + 8 * (4 * a + c)), 8), :]
                        for a in (pa, pa + 2)
                        for c in range(4)
                    }
                    for a in (pa, pa + 2):
                        for b in (pb, pb + 2):
                            gz = [
                                g[pl.ds(gat + (2560 + 640 * pc + 8 * (4 * a + b)), 8), :]
                                for pc in range(2)
                            ]
                            for c in range(4):
                                row = 8 * PLACE[a, b, c]
                                n = gx[b, c] + gy[a, c] + gz[c % 2]
                                image = tr[pl.ds(at + row, 8), :] - scaled * n
                                store((at, row), level(a, b, c), image)
            return carry

        lax.fori_loop(0, FIELDS, field, 0)

    def ld(ref, row, start=0, more=0):
        return ref[pl.ds(pl.multiple_of(start + row[0], 256) + (more + row[1]), 8), :]

    def put(ref, row, x, start=0, more=0):
        ref[pl.ds(pl.multiple_of(start + row[0], 256) + (more + row[1]), 8), :] = x

    def tab(ref, i):
        return ref[8 * i : 8 * i + 8, :]

    def kind_0(t):
        def store(row, i, image):
            put(gg, row, image)
            start = ld(ss, row)
            put(tt, row, start)
            put(vv, row, tab(dh, i) * (start - image), 0, work)

        finish(store)

    def kind_1(t):
        def store(row, i, image):
            put(vv, row, tab(dh, i) * (ld(ss, row) - image), 0, work)

        finish(store)

    def kind_2(t):
        def store(row, i, image):
            u = tab(dh, i) * (ld(ss, row) - image)
            put(first, row, u)
            put(vv, row, tab(dh, i) * (u - ld(gg, row)), 0, work)

        finish(store)

    def kind_3(t):
        def store(row, i, image):
            put(vv, row, tab(dh, i) * (ld(first, row) - image), 0, work)

        finish(store)

    def kind_4(t):
        def store(row, i, image):
            u1 = ld(first, row)
            u2 = tab(dh, i) * (u1 - image)
            start = ld(ss, row)
            put(vv, row, u1 - 0.5 * (start + u2), 0, mid)
            mix = (4.0 / 3.0) * u1 + (1.0 / 3.0) * u2
            put(vv, row, mix, 0, work)
            q = u2 + u2 - mix
            put(quad, row, q)
            put(base, row, tab(el, i) * (q - (1.0 / 3.0) * start) - (1.0 / 3.0) * ld(gg, row))

        finish(store)

    def kind_5(t):
        def store(row, i, image):
            z = ld(base, row) - image
            rest = tab(de, i) * z - ld(quad, row)
            put(zed, row, rest)
            put(vv, row, tab(de, i) * ld(ss, row) + rest, 0, work)

        finish(store)

    def kind_6(t):
        def store(row, i, image):
            put(hga, row, image)
            c = (1.0 / 3.0) * (tab(el, i) * ld(vv, row, 0, mid) + image)
            put(c0, row, c)
            put(c2, row, c + c)

        finish(store)

    def kind_7(t):
        at = t * SIZE

        def store(row, i, image):
            s = tab(dd, i) * (ld(ss, row, at) + ld(base, row) - image)
            put(ss, row, s, at, SIZE)
            put(vv, row, s, 0, copy)
            put(vv, row, tab(de, i) * s + ld(zed, row), 0, work)

        finish(store)

    def kind_8(t):
        at = t * SIZE

        def store(row, i, image):
            put(gg, row, image, at, SIZE)
            s = ld(ss, row, at)
            old = ld(gg, row, at)
            phi = 0.25 * (tab(el, i) * (ld(ss, row, at, SIZE) - s) + image - old)
            target = s + phi + ld(c0, row)
            put(tt, row, target, at, SIZE)
            put(pp, row, phi - ld(c2, row), at)
            put(vv, row, tab(dh, i) * (target - ld(hga, row) - 0.5 * (old + image)), at)

        finish(store)

    def kind_9(t):
        at = t * SIZE

        def store(row, i, image):
            put(vv, row, tab(dh, i) * (ld(tt, row, at, SIZE) - image), at)

        finish(store)

    def kind_10(t):
        at = t * SIZE

        def store(row, i, image):
            u = tab(dh, i) * (ld(tt, row, at, SIZE) - image)
            put(uu, row, u, at)
            target = u + ld(pp, row, at)
            put(tt, row, target, at, SIZE)
            put(vv, row, tab(dh, i) * (target - ld(gg, row, at, SIZE)), at)

        finish(store)

    def kind_11(t):
        at = t * SIZE

        def store(row, i, image):
            u1 = ld(uu, row, at)
            u2 = tab(dh, i) * (ld(tt, row, at, SIZE) - image)
            s = ld(ss, row, at)
            mix = (4.0 / 3.0) * u1 + (1.0 / 3.0) * u2
            put(vv, row, mix, at)
            q = u2 + u2 - mix
            put(pp, row, q, at)
            old = ld(gg, row, at)
            put(tt, row, tab(el, i) * (q - (1.0 / 3.0) * s) - (1.0 / 3.0) * old, at, SIZE)

        finish(store)

    def kind_12(t):
        at = t * SIZE

        def store(row, i, image):
            z = ld(tt, row, at, SIZE) - image
            rest = tab(de, i) * z - ld(pp, row, at)
            put(gg, row, rest, at)
            put(vv, row, tab(de, i) * ld(ss, row) + rest, 0, work)

        finish(store)

    def kind_13(t):
        at = t * SIZE
        later = jnp.minimum(t + 1, slices - 1) * SIZE

        def store(row, i, image):
            s = tab(dd, i) * (ld(tt, row, at) + ld(tt, row, at, SIZE) - image)
            put(tt, row, s, at, SIZE)
            put(vv, row, tab(de, i) * s + ld(gg, row, later), 0, work)

        finish(store)

    kinds = [kind_9, kind_8, kind_7, kind_10, kind_11, kind_12, kind_13]
    kinds += [kind_0, kind_1, kind_2, kind_3, kind_4, kind_5, kind_6]

    def step(n, carry):
        at = [pl.multiple_of(plan[5 * n + i], SIZE) for i in range(1, 4)]
        one, other = transport(at[0]), faces(*at)
        for _ in other:
            next(one, None)
        lax.switch(plan[5 * n], kinds, plan[5 * n + 4])
        return carry

    lax.fori_loop(0, len(steps(slices)), step, 0)

    for f in range(FIELDS):

        def own(ref, slot):
            at = slot * SIZE + f * 256 + column
            return jnp.concatenate([ref[pl.ds(at + 1280 * p, 32, 8), :] for p in (0, 1)], axis=0)

        begin, end = own(tt, mine), own(tt, mine + 1)
        fine_end = 0.5 * (own(pp, mine) + own(vv, mine))
        middle = own(uu, mine) + 0.5 * (begin - own(ss, mine) + end - fine_end)
        x = jnp.concatenate([begin, middle, end], axis=1)
        r = jnp.dot(back[...], split_rows(x), preferred_element_type=f32)
        for i in range(3):
            out[i, 64 * f : 64 * f + 64, :] = r[:, 128 * i : 128 * i + 128]


def join_kernel(values, viscosity, out):
    out[0:ROWS, :] = values[...]
    out[ROWS : ROWS + 8, :] = jnp.broadcast_to(viscosity[...], (8, 128))


def local_whole_grid(slices):
    def local(initial, viscosity, flux_jacobian):
        vmem = pl.BlockSpec(memory_space=pltpu.VMEM)
        block = pl.pallas_call(
            join_kernel,
            out_shape=jax.ShapeDtypeStruct((ROWS + 8, 128), jnp.float32),
            in_specs=[vmem, vmem],
            out_specs=vmem,
        )(initial.reshape(ROWS, 128), viscosity.reshape(1, 128))
        near = [block]
        for k in range(1, 4):
            near.append(lax.ppermute(block, "sy", [(i, i ^ k) for i in range(4)]))
        gathered = near + [lax.ppermute(b, "sx", [(0, 1), (1, 0)]) for b in near]

        plan = [(ORDER.index(kind), at * SIZE, at * SIZE, at * SIZE, t) for kind, at, t in steps(slices)]
        plan = jnp.asarray(np.array(plan, np.int32).reshape(-1))

        into, back, blocks = modal_tables()
        tables = jnp.asarray(blocks, jnp.float32)
        matrix = sum(
            flux_jacobian[d][None, :, None, :, None] * tables[:, d, None, :, None, :] for d in range(3)
        ).reshape(2, 160, 160)

        smem = pl.BlockSpec(memory_space=pltpu.SMEM)
        hbm = pl.BlockSpec(memory_space=pltpu.HBM)

        def scratch(rows):
            return pltpu.VMEM((rows, 128), jnp.float32)

        out = pl.pallas_call(
            lambda plan, *refs: whole_grid_kernel(slices, plan, *refs),
            out_shape=jax.ShapeDtypeStruct((3, ROWS, 128), jnp.float32),
            in_specs=[smem] + [hbm] * 8 + [vmem] * 3,
            out_specs=vmem,
            scratch_shapes=[
                scratch((slices + 1) * SIZE),
                scratch((slices + 1) * SIZE),
                scratch((slices + 1) * SIZE),
                scratch(slices * SIZE),
                scratch((slices + 3) * SIZE),
                scratch(slices * SIZE),
                *[scratch(SIZE)] * 7,
                scratch(SIZE),
                scratch(3840),
                pltpu.VMEM((2, 160, 480), jnp.bfloat16),
                *[scratch(8 * len(LEVELS))] * 4,
                scratch(8),
                pltpu.VMEM((8, ROWS + 8, 128), jnp.float32),
                pltpu.SemaphoreType.DMA((8,)),
            ],
            compiler_params=pltpu.CompilerParams(vmem_limit_bytes=58 << 20),
        )(plan, *gathered, matrix, three_pass(into), three_pass(back))
        return out.reshape(1, 3, 1, 1, FIELDS, 64, 128)

    return local


def solution(mesh):
    grid = (mesh.shape["sx"], mesh.shape["sy"])
    slices = mesh.shape["tm"]
    local = local_whole_grid(slices) if grid == (2, 4) and slices <= 4 else local_exchanging
    return jax.shard_map(
        local,
        mesh=mesh,
        in_specs=(P("sx", "sy", None, None, None), P("sx", "sy", None), P()),
        out_specs=P("tm", None, "sx", "sy", None, None, None),
        check_vma=False,
    )
```
